128 devices in a mesh: branch: 2 (over x_hi), ulysses: 4 (over y), fsdp: 16 (over z, x_lo, core).
Axes of the slice: x: 4 (x_hi: 2, x_lo: 2; x = x_hi * 2 + x_lo), y: 4, z: 4, core: 2. Of those that a mesh axis runs over, the one named last changes fastest.
Arguments:
- hidden: bfloat16 [2, 16, 1024, 5120], P('branch', 'fsdp', 'ulysses'), may hold values from -128 to 128, as said below
- query: bfloat16 [2, 16, 1024, 2560], P('branch', 'fsdp', None, 'ulysses'), may hold values from -128 to 128, as said below
- key: bfloat16 [2, 16, 1024, 2560], P('branch', 'fsdp', None, 'ulysses'), may hold values from -5 to 5, as said below
- value: bfloat16 [2, 16, 1024, 2560], P('branch', 'fsdp', None, 'ulysses'), may hold values from -6 to 6
- output_projection_weight: bfloat16 [2560, 5120], P('fsdp'), may hold values from -0.125 to 0.125
- adapter_down_weight: bfloat16 [2560, 64], replicated, may hold values from -0.125 to 0.125
- adapter_up_weight: bfloat16 [64, 5120], replicated, may hold values from -0.75 to 0.75
- reward_gradient: bfloat16 [16, 1024, 5120], P('fsdp', 'ulysses'), may hold values from -24 to 24, as said below
Outputs:
- grad_hidden: bfloat16 [2, 16, 1024, 5120], P('branch', 'fsdp', 'ulysses')
- grad_query: bfloat16 [2, 16, 1024, 2560], P('branch', 'fsdp', None, 'ulysses')
- grad_key: bfloat16 [2, 16, 1024, 2560], P('branch', 'fsdp', None, 'ulysses')
- grad_value: bfloat16 [2, 16, 1024, 2560], P('branch', 'fsdp', None, 'ulysses')
- adapter_down_gradient: float32 [2560, 64], replicated
- adapter_up_gradient: float32 [64, 5120], replicated
The draws below stay inside these ranges and needn't reach their ends.
Inputs may be any that keep to these rules, and one draw needn't show every extreme that they name: `hidden`: Real-valued residual stream. `query`: Real-valued queries. `key`: Real-valued keys. `reward_gradient`: Real-valued reward gradient.
All inputs are finite; a program needn't handle non-finite values.
Results may differ from the reference program's by a relative error of at most 0.013.
Values may be sent and summed in bfloat16 or wider, within the bound.
No kernel may reach another device: no remote copies, remote signals or barrier semaphores. Data moves between devices by JAX's collectives and lax.ppermute only.
A program may use at most 192 MiB of HBM per device.

```python
import jax
import jax.numpy as jnp
from jax import lax

MODEL_DIM = 5120
HEADS = 20
HD = 128
ADAPTER_RANK = 64
ATTEND_FEATURES = 2560
SEQ = 1024
BATCH = 16


def shared_field(key):
    key_base, key_rows, key_cols = jax.random.split(key, 3)
    base = jnp.clip(jax.random.normal(key_base, (BATCH, SEQ, MODEL_DIM), jnp.float32), -4.0, 4.0)
    row_scale = jnp.exp(jax.random.uniform(key_rows, (BATCH, SEQ, 1), jnp.float32, -1.15, 1.15))
    col_scale = jnp.exp(jax.random.uniform(key_cols, (1, 1, MODEL_DIM), jnp.float32, -1.15, 1.15))
    ramp = 0.6 + 1.2 * jnp.arange(SEQ, dtype=jnp.float32).reshape(1, SEQ, 1) / max(SEQ - 1, 1)
    return base * row_scale * col_scale * ramp


def head_field(key):
    return jnp.clip(jax.random.normal(key, (2, BATCH, SEQ, ATTEND_FEATURES), jnp.float32), -5.0, 5.0)


def draw_hidden(key, part):
    common = shared_field(key)
    key = jax.random.fold_in(key, 3)
    own_part = jnp.clip(jax.random.normal(key, (2, BATCH, SEQ, MODEL_DIM), jnp.float32), -4.0, 4.0)
    return (common[None] + 0.5 * own_part).astype(jnp.bfloat16)


def draw_reward_gradient(key, part):
    common = shared_field(key)
    key = jax.random.fold_in(key, 5)
    noise = jnp.clip(jax.random.normal(key, (BATCH, SEQ, MODEL_DIM), jnp.float32), -4.0, 4.0)
    return (0.12 * common + 0.2 * noise).astype(jnp.bfloat16)


def draw_key(key, part):
    base = head_field(key)
    return base.astype(jnp.bfloat16)


def draw_query(key, part):
    key = jax.random.fold_in(key, 9)
    own_part = 1.5 * jnp.clip(jax.random.normal(key, (2, BATCH, SEQ, ATTEND_FEATURES), jnp.float32), -5.0, 5.0)
    return own_part.astype(jnp.bfloat16)


def block_scale(key, extent, cuts, smallest, top_value):
    gain, own = 1.0, jax.random.fold_in(key, 6)
    for axis_at, blocks in cuts:
        heights = jnp.exp(jax.random.uniform(jax.random.fold_in(own, axis_at), (blocks,), jnp.float32, smallest / len(cuts), top_value / len(cuts)))
        gain = gain * jnp.repeat(heights, extent[axis_at] // blocks).reshape([-1 if axis == axis_at else 1 for axis in range(len(extent))])
    return gain


def scatter_about(rng, shape, scale, most, cuts=(), held_as=jnp.bfloat16):
    entries = scale * jax.random.normal(rng, shape, jnp.float32)
    if cuts:
        entries = entries * block_scale(rng, shape, cuts, -0.22, 0.18)
    return jnp.clip(entries, -most, most).astype(held_as)


def setup_inputs(seed: int = 0) -> dict:
    keys = jax.random.split(jax.random.key(seed), 9)
    return {
        "hidden": draw_hidden(jax.random.fold_in(keys[8], 71), 0),
        "query": draw_query(jax.random.fold_in(keys[8], 71), 0),
        "key": draw_key(jax.random.fold_in(keys[8], 71), 0),
        "value": scatter_about(keys[3], (2, BATCH, SEQ, ATTEND_FEATURES), 1.0, 6.0, ((0, 2), (1, 16), (3, 4))),
        "output_projection_weight": scatter_about(keys[4], (ATTEND_FEATURES, MODEL_DIM), ATTEND_FEATURES ** -0.5, 0.125, ((0, 16),)),
        "adapter_down_weight": scatter_about(keys[5], (ATTEND_FEATURES, ADAPTER_RANK), ATTEND_FEATURES ** -0.5, 0.125),
        "adapter_up_weight": scatter_about(keys[6], (ADAPTER_RANK, MODEL_DIM), ADAPTER_RANK ** -0.5, 0.75),
        "reward_gradient": draw_reward_gradient(jax.random.fold_in(keys[8], 71), 0),
    }


GUIDANCE = 5.0


def head_form(tensor):
    branch_count, batch_count, seq_len, feature_count = tensor.shape
    shaped = tensor.reshape(branch_count, batch_count, seq_len, HEADS, HD)
    return shaped.transpose(0, 1, 3, 2, 4).reshape(branch_count * batch_count * HEADS, seq_len, HD)


def token_form(tensor, branch_count, batch_count):
    seq_len = tensor.shape[1]
    shaped = tensor.reshape(branch_count, batch_count, HEADS, seq_len, HD)
    return shaped.transpose(0, 1, 3, 2, 4).reshape(branch_count, batch_count, seq_len, HEADS * HD)


def softmax_probs(query_head, key_head, score_scale):
    scores = jnp.dot(query_head, key_head.T, preferred_element_type=jnp.float32) * score_scale
    row_peak = jnp.max(scores, axis=1, keepdims=True)
    exp_scores = jnp.exp(scores - row_peak)
    return exp_scores / jnp.sum(exp_scores, axis=1, keepdims=True)


def reference(hidden, query, key, value, output_projection_weight, adapter_down_weight, adapter_up_weight, reward_gradient):
    score_scale = HD ** -0.5
    branch_count, batch_count = hidden.shape[0], hidden.shape[1]
    query_heads = head_form(query)
    key_heads = head_form(key)
    value_heads = head_form(value)

    def forward_one(head_items):
        query_head, key_head, value_head = head_items
        attn_probs = softmax_probs(query_head, key_head, score_scale)
        return jnp.dot(attn_probs.astype(jnp.bfloat16), value_head, preferred_element_type=jnp.float32).astype(jnp.bfloat16)

    attended_heads = lax.map(forward_one, (query_heads, key_heads, value_heads))
    attention_output = token_form(attended_heads, branch_count, batch_count)
    flattened_attention = attention_output.reshape(-1, ATTEND_FEATURES)
    adapter_middle = jnp.dot(flattened_attention, adapter_down_weight, preferred_element_type=jnp.float32).astype(jnp.bfloat16)
    guided_velocity = hidden.reshape(-1, MODEL_DIM).astype(jnp.float32)
    guided_velocity = guided_velocity + jnp.dot(flattened_attention, output_projection_weight, preferred_element_type=jnp.float32)
    guided_velocity = guided_velocity + jnp.dot(adapter_middle, adapter_up_weight, preferred_element_type=jnp.float32)
    guided_velocity = guided_velocity.astype(jnp.bfloat16).reshape(hidden.shape)

    cond_velocity = guided_velocity[0].astype(jnp.float32)
    uncond = guided_velocity[1].astype(jnp.float32)
    target = reward_gradient.astype(jnp.float32)
    inner_sum = jnp.sum(cond_velocity * uncond, axis=(1, 2))
    energy = jnp.sum(uncond * uncond, axis=(1, 2)) + 1e-8
    pull_sum = jnp.sum(target * uncond, axis=(1, 2))
    cfg_scale = inner_sum / energy
    cfg_slope = (1.0 - GUIDANCE) * pull_sum / energy
    grad_cond = GUIDANCE * target + cfg_slope[:, None, None] * uncond
    target_coef = ((1.0 - GUIDANCE) * cfg_scale)[:, None, None]
    uncond_coef = (-2.0 * cfg_slope * cfg_scale)[:, None, None]
    grad_uncond = target_coef * target + cfg_slope[:, None, None] * cond_velocity + uncond_coef * uncond
    grad_hidden = jnp.stack([grad_cond, grad_uncond]).astype(jnp.bfloat16)

    flattened_gradient = grad_hidden.reshape(-1, MODEL_DIM)
    middle_gradient = jnp.dot(flattened_gradient, adapter_up_weight.T, preferred_element_type=jnp.float32).astype(jnp.bfloat16)
    adapter_up_gradient = jnp.dot(adapter_middle.T, flattened_gradient, preferred_element_type=jnp.float32)
    adapter_down_gradient = jnp.dot(flattened_attention.T, middle_gradient, preferred_element_type=jnp.float32)
    attention_gradient = jnp.dot(flattened_gradient, output_projection_weight.T, preferred_element_type=jnp.float32)
    attention_gradient = attention_gradient + jnp.dot(middle_gradient, adapter_down_weight.T, preferred_element_type=jnp.float32)
    attention_gradient = attention_gradient.astype(jnp.bfloat16).reshape(attention_output.shape)
    grad_heads = head_form(attention_gradient)

    def backward_one(head_items):
        query_head, key_head, value_head, output_head, grad_head = head_items
        attn_probs = softmax_probs(query_head, key_head, score_scale)
        row_delta = jnp.sum(grad_head.astype(jnp.float32) * output_head.astype(jnp.float32), axis=1, keepdims=True)
        grad_probs = jnp.dot(grad_head, value_head.T, preferred_element_type=jnp.float32)
        grad_scores = (attn_probs * (grad_probs - row_delta)).astype(jnp.bfloat16)
        grad_value_head = jnp.dot(attn_probs.astype(jnp.bfloat16).T, grad_head, preferred_element_type=jnp.float32).astype(jnp.bfloat16)
        grad_query_head = (jnp.dot(grad_scores, key_head, preferred_element_type=jnp.float32) * score_scale).astype(jnp.bfloat16)
        grad_key_head = (jnp.dot(grad_scores.T, query_head, preferred_element_type=jnp.float32) * score_scale).astype(jnp.bfloat16)
        return grad_query_head, grad_key_head, grad_value_head

    grad_query_heads, grad_key_heads, grad_value_heads = lax.map(
        backward_one, (query_heads, key_heads, value_heads, attended_heads, grad_heads))
    return (grad_hidden,
            token_form(grad_query_heads, branch_count, batch_count),
            token_form(grad_key_heads, branch_count, batch_count),
            token_form(grad_value_heads, branch_count, batch_count),
            adapter_down_gradient,
            adapter_up_gradient)
```

```python
import functools

import jax
import jax.numpy as jnp
from jax import lax
from jax.experimental import pallas as pl
from jax.experimental.pallas import tpu as pltpu
from jax.sharding import PartitionSpec as P

HD = 128
GUIDANCE = 5.0
SCALE = HD ** (-0.5)
VMEM = 56 * 1024 * 1024
LAST = (((1,), (1,)), ((), ()))
FIRST = (((0,), (0,)), ((), ()))
F32 = jnp.float32
BF16 = jnp.bfloat16


def dot(a, b, dims=(((1,), (0,)), ((), ()))):
    return lax.dot_general(a, b, dims, preferred_element_type=F32)


def params():
    return pltpu.CompilerParams(vmem_limit_bytes=VMEM)


def forward_kernel(q_ref, k_ref, v_ref, p_ref, o_ref):
    rows = o_ref.shape[2]
    for part in range(o_ref.shape[1]):
        at = pl.ds(part * rows, rows)
        scores = dot(q_ref[at, :], k_ref[...], LAST) * SCALE
        exps = jnp.exp(scores - jnp.max(scores, axis=1, keepdims=True))
        probs = (exps / jnp.sum(exps, axis=1, keepdims=True)).astype(BF16)
        p_ref[0, at, :] = probs
        out = dot(probs, v_ref[...]).astype(BF16)
        o_ref[0, part] = out
        o_ref[1, part] = out


def attention_forward(query, key, value, parts):
    seq, width = query.shape
    heads = width // HD
    block = pl.BlockSpec((seq, HD), lambda h: (0, h))
    return pl.pallas_call(
        forward_kernel,
        grid=(heads,),
        in_specs=[block] * 3,
        out_specs=[
            pl.BlockSpec((1, seq, seq), lambda h: (h, 0, 0)),
            pl.BlockSpec((2, parts, seq // parts, HD), lambda h: (0, 0, 0, h)),
        ],
        out_shape=[
            jax.ShapeDtypeStruct((heads, seq, seq), BF16),
            jax.ShapeDtypeStruct((2, parts, seq // parts, width), BF16),
        ],
        compiler_params=params(),
        cost_estimate=pl.CostEstimate(
            flops=heads * 8 * seq * seq * HD,
            bytes_accessed=heads * seq * seq * 2,
            transcendentals=heads * seq * seq,
        ),
    )(query, key, value)


def backward_kernel(p_ref, q_ref, k_ref, v_ref, o_ref, g_ref, dq_ref, dk_ref, dv_ref):
    seq = q_ref.shape[0]
    probs = p_ref[0]
    grad32 = g_ref[0].astype(F32) + g_ref[1].astype(F32)
    grad32 = grad32.reshape(seq, HD)
    grad = grad32.astype(BF16)
    out = o_ref[0].reshape(seq, HD).astype(F32)
    delta = jnp.sum(grad.astype(F32) * out, axis=1, keepdims=True)
    grad_probs = dot(grad, v_ref[...], LAST)
    grad_scores = (probs.astype(F32) * (grad_probs - delta)).astype(BF16)
    dv_ref[...] = dot(probs, grad, FIRST).astype(BF16)
    dq_ref[...] = (dot(grad_scores, k_ref[...]) * SCALE).astype(BF16)
    dk_ref[...] = (dot(grad_scores, q_ref[...], FIRST) * SCALE).astype(BF16)


def attention_backward(probs, query, key, value, out, grads):
    seq, width = query.shape
    heads = width // HD
    parts = out.shape[1]
    block = pl.BlockSpec((seq, HD), lambda h: (0, h))
    return pl.pallas_call(
        backward_kernel,
        grid=(heads,),
        in_specs=[
            pl.BlockSpec((1, seq, seq), lambda h: (h, 0, 0)),
            block,
            block,
            block,
            pl.BlockSpec((1, parts, seq // parts, HD), lambda h: (0, 0, 0, h)),
            pl.BlockSpec((2, parts, seq // parts, HD), lambda h: (0, 0, 0, h)),
        ],
        out_specs=[block] * 3,
        out_shape=[jax.ShapeDtypeStruct((seq, width), BF16)] * 3,
        compiler_params=params(),
        cost_estimate=pl.CostEstimate(
            flops=heads * 16 * seq * seq * HD,
            bytes_accessed=heads * seq * seq * 2,
            transcendentals=0,
        ),
    )(probs, query, key, value, out, grads)


def velocity_kernel(
    b_ref, a_ref, w_ref, hown_ref, hoth_ref, r_ref, down_ref, up_ref,
    v_ref, m_ref, sum_ref, x_scr, m_scr, s_scr,
):
    step = pl.program_id(0)
    tokens = hown_ref.shape[0]
    wide = a_ref.shape[3]

    @pl.when(step == 0)
    def _():
        for u in range(a_ref.shape[1]):
            for b in range(2):
                x_scr[pl.ds(b * tokens, tokens), pl.ds(u * wide, wide)] = a_ref[b, u]
        mid = dot(x_scr[...], down_ref[...]).astype(BF16)
        m_scr[...] = mid
        m_ref[...] = mid.reshape(m_ref.shape)
        s_scr[...] = jnp.zeros_like(s_scr)

    first = b_ref[0] == 0
    own, oth = hown_ref[...].astype(F32), hoth_ref[...].astype(F32)
    acc = dot(x_scr[...], w_ref[...]) + dot(m_scr[...], up_ref[...])
    cond = (jnp.where(first, own, oth) + acc[:tokens]).astype(BF16)
    uncond = (jnp.where(first, oth, own) + acc[tokens:]).astype(BF16)
    v_ref[0] = cond
    v_ref[1] = uncond
    c32, u32, r32 = cond.astype(F32), uncond.astype(F32), r_ref[...].astype(F32)
    for row, term in enumerate((c32 * u32, u32 * u32, r32 * u32)):
        s_scr[pl.ds(row, 1), :] += jnp.sum(term, axis=0, keepdims=True)

    @pl.when(step == pl.num_programs(0) - 1)
    def _():
        totals = jnp.sum(s_scr[...], axis=1, keepdims=True)
        lane = lax.broadcasted_iota(jnp.int32, sum_ref.shape, 1)
        sum_ref[...] = jnp.where(
            lane == 0, totals[0:1], jnp.where(lane == 1, totals[1:2], totals[2:3])
        )


def velocity(branch, attended, weight, hidden, hidden_other, reward, down, up, copies):
    tokens, half = hidden_other.shape
    depth, rank = down.shape
    tile = 512
    steps = half // tile
    mine = lambda j, b: (0, b[0] * steps + j)
    return pl.pallas_call(
        velocity_kernel,
        grid_spec=pltpu.PrefetchScalarGridSpec(
            num_scalar_prefetch=1,
            grid=(steps,),
            in_specs=[
                pl.BlockSpec(attended.shape, lambda j, b: (0, 0, 0, 0)),
                pl.BlockSpec((depth, tile), lambda j, b: (0, j)),
                pl.BlockSpec((tokens, tile), mine),
                pl.BlockSpec((tokens, tile), lambda j, b: (0, j)),
                pl.BlockSpec((tokens, tile), mine),
                pl.BlockSpec((depth, rank), lambda j, b: (0, 0)),
                pl.BlockSpec((rank, tile), mine),
            ],
            out_specs=[
                pl.BlockSpec((2, tokens, tile), lambda j, b: (0, 0, j)),
                pl.BlockSpec((2, tokens, rank), lambda j, b: (0, 0, 0)),
                pl.BlockSpec((8 * copies, 128), lambda j, b: (0, 0)),
            ],
            scratch_shapes=[
                pltpu.VMEM((2 * tokens, depth), BF16),
                pltpu.VMEM((2 * tokens, rank), BF16),
                pltpu.VMEM((8, tile), F32),
            ],
        ),
        out_shape=[
            jax.ShapeDtypeStruct((2, tokens, half), BF16),
            jax.ShapeDtypeStruct((2, tokens, rank), BF16),
            jax.ShapeDtypeStruct((8 * copies, 128), F32),
        ],
        compiler_params=params(),
        cost_estimate=pl.CostEstimate(
            flops=4 * tokens * depth * half,
            bytes_accessed=2 * depth * half,
            transcendentals=0,
        ),
    )(branch, attended, weight, hidden, hidden_other, reward, down, up)


def gradient_kernel(
    b_ref, v_ref, r_ref, sum_ref, w_ref, down_ref, up_ref,
    own_ref, oth_ref, mid_ref, g_ref, x_scr, m_scr,
):
    tokens = r_ref.shape[0]

    @pl.when(pl.program_id(0) == 0)
    def _():
        totals = sum_ref[0:1, :]
        for at in range(8, sum_ref.shape[0], 8):
            totals = totals + sum_ref[at : at + 1, :]
        inner, energy, pull = totals[:, 0:1], totals[:, 1:2] + 1e-08, totals[:, 2:3]
        scale = inner / energy
        slope = (1.0 - GUIDANCE) * pull / energy
        first = b_ref[0] == 0
        tile = 512
        for at in range(0, r_ref.shape[1], tile):
            cols = pl.ds(at, tile)
            target = r_ref[:, cols].astype(F32)
            cond = v_ref[0, :, cols].astype(F32)
            uncond = v_ref[1, :, cols].astype(F32)
            grad0 = (GUIDANCE * target + slope * uncond).astype(BF16)
            grad1 = (
                ((1.0 - GUIDANCE) * scale) * target
                + slope * cond
                + (-2.0 * slope * scale) * uncond
            ).astype(BF16)
            x_scr[0:tokens, cols] = grad0
            x_scr[tokens : 2 * tokens, cols] = grad1
            own_ref[:, cols] = jnp.where(first, grad0, grad1)
            oth_ref[:, cols] = jnp.where(first, grad1, grad0)
        mid = dot(x_scr[...], up_ref[...], LAST).astype(BF16)
        m_scr[...] = mid
        mid_ref[...] = mid.reshape(mid_ref.shape)

    part = dot(x_scr[...], w_ref[...], LAST) + dot(m_scr[...], down_ref[...], LAST)
    g_ref[...] = part.astype(BF16).reshape(g_ref.shape)


def gradient(branch, vel, reward, sums, weight, down, up, parts):
    _, tokens, half = vel.shape
    depth, rank = down.shape
    wide = depth // parts
    whole = lambda j, b: (0, 0)
    mine = lambda j, b: (0, b[0])
    return pl.pallas_call(
        gradient_kernel,
        grid_spec=pltpu.PrefetchScalarGridSpec(
            num_scalar_prefetch=1,
            grid=(parts,),
            in_specs=[
                pl.BlockSpec((2, tokens, half), lambda j, b: (0, 0, 0)),
                pl.BlockSpec((tokens, half), mine),
                pl.BlockSpec(sums.shape, whole),
                pl.BlockSpec((wide, half), lambda j, b: (j, 0)),
                pl.BlockSpec((wide, rank), lambda j, b: (j, 0)),
                pl.BlockSpec((rank, half), mine),
            ],
            out_specs=[
                pl.BlockSpec((tokens, half), whole),
                pl.BlockSpec((tokens, half), whole),
                pl.BlockSpec((2, tokens, rank), lambda j, b: (0, 0, 0)),
                pl.BlockSpec((2, 1, tokens, wide), lambda j, b: (0, j, 0, 0)),
            ],
            scratch_shapes=[
                pltpu.VMEM((2 * tokens, half), BF16),
                pltpu.VMEM((2 * tokens, rank), BF16),
            ],
        ),
        out_shape=[
            jax.ShapeDtypeStruct((tokens, half), BF16),
            jax.ShapeDtypeStruct((tokens, half), BF16),
            jax.ShapeDtypeStruct((2, tokens, rank), BF16),
            jax.ShapeDtypeStruct((2, parts, tokens, wide), BF16),
        ],
        compiler_params=params(),
        cost_estimate=pl.CostEstimate(
            flops=4 * tokens * depth * half,
            bytes_accessed=2 * depth * half,
            transcendentals=0,
        ),
    )(branch, vel, reward, sums, weight, down, up)


def exchange(block, axes):
    return lax.all_to_all(block, axes, split_axis=0, concat_axis=0, tiled=True)


def swap(block):
    return lax.ppermute(block, "branch", [(0, 1), (1, 0)])


def body(
    hidden,
    query,
    key,
    value,
    output_projection_weight,
    adapter_down_weight,
    adapter_up_weight,
    reward_gradient,
):
    parts = lax.axis_size("ulysses")
    clips = lax.axis_size("fsdp")
    branch = lax.axis_index("branch")
    branch_word = branch.reshape(1).astype(jnp.int32)
    _, _, tokens, model = hidden.shape
    half = model // 2
    _, _, seq, width = query.shape
    depth, rank = adapter_down_weight.shape
    query2, key2, value2 = (a.reshape(seq, width) for a in (query, key, value))
    hidden2 = hidden.reshape(tokens, model)
    reward2 = reward_gradient.reshape(tokens, model)

    own_columns = lax.dynamic_slice_in_dim(output_projection_weight, branch * half, half, 1)
    weight = lax.all_gather(own_columns, "fsdp", axis=0, tiled=True)
    hidden_other = swap(lax.dynamic_slice_in_dim(hidden2, (1 - branch) * half, half, 1))

    probs, attended = attention_forward(query2, key2, value2, parts)
    gathered = exchange(attended.reshape(2 * seq, width), ("branch", "ulysses"))
    gathered = gathered.reshape(2, parts, tokens, width)

    vel, middle, sums = velocity(
        branch_word, gathered, weight, hidden2, hidden_other, reward2,
        adapter_down_weight, adapter_up_weight, 2 * parts,
    )
    sums = exchange(sums, ("branch", "ulysses"))
    grad_own, grad_other, grad_middle, grad_part = gradient(
        branch_word, vel, reward2, sums, weight, adapter_down_weight, adapter_up_weight, parts
    )
    grads = exchange(grad_part.reshape(2 * seq, width), ("branch", "ulysses"))
    grads = grads.reshape(2, parts, tokens, width)

    down_part = jnp.einsum("btk,butf->kuf", grad_middle, gathered, preferred_element_type=F32)
    mine = lax.dynamic_index_in_dim(middle, branch, 0, keepdims=False)
    other = lax.dynamic_index_in_dim(middle, 1 - branch, 0, keepdims=False)
    up_part = dot(mine, grad_own, FIRST) + dot(other, grad_other, FIRST)
    both = jnp.concatenate([down_part.reshape(rank, depth), up_part], axis=0).astype(BF16)
    group = 8
    rows = 2 * rank // group
    lanes = parts * clips // rows
    piece = half // lanes
    both = both.reshape(rows, group, lanes, piece).transpose(0, 2, 1, 3)
    both = exchange(both.reshape(rows * lanes * group, piece), ("ulysses", "fsdp"))
    total = jnp.sum(both.reshape(rows * lanes, group, piece).astype(F32), axis=0)
    partner = swap(total)
    cond_total = jnp.where(branch == 0, total, partner)
    uncond_total = jnp.where(branch == 0, partner, total)
    packed = jnp.concatenate([cond_total, uncond_total], axis=0).astype(BF16)
    packed = jnp.broadcast_to(packed[None], (rows * lanes, 2 * group, piece))
    packed = exchange(packed.reshape(rows * lanes * 2 * group, piece), ("ulysses", "fsdp"))
    packed = packed.reshape(rows, lanes, 2, group, piece).transpose(2, 0, 3, 1, 4)
    packed = packed.reshape(2, 2 * rank, half).astype(F32)
    adapter_down_gradient = (packed[0, :rank] + packed[1, :rank]).T
    adapter_up_gradient = jnp.concatenate([packed[0, rank:], packed[1, rank:]], axis=1)

    received = swap(grad_other)
    grad_hidden = jnp.where(
        branch == 0,
        jnp.concatenate([grad_own, received], axis=1),
        jnp.concatenate([received, grad_own], axis=1),
    )
    grad_query, grad_key, grad_value = attention_backward(
        probs, query2, key2, value2, attended, grads
    )
    return (
        grad_hidden.reshape(hidden.shape),
        grad_query.reshape(query.shape),
        grad_key.reshape(key.shape),
        grad_value.reshape(value.shape),
        adapter_down_gradient,
        adapter_up_gradient,
    )


def solution(mesh):
    in_specs = (
        P("branch", "fsdp", "ulysses", None),
        P("branch", "fsdp", None, "ulysses"),
        P("branch", "fsdp", None, "ulysses"),
        P("branch", "fsdp", None, "ulysses"),
        P("fsdp", None),
        P(),
        P(),
        P("fsdp", "ulysses", None),
    )
    out_specs = (
        P("branch", "fsdp", "ulysses", None),
        P("branch", "fsdp", None, "ulysses"),
        P("branch", "fsdp", None, "ulysses"),
        P("branch", "fsdp", None, "ulysses"),
        P(),
        P(),
    )
    return jax.shard_map(body, mesh=mesh, in_specs=in_specs, out_specs=out_specs, check_vma=False)
```

```python
import functools

import jax
import jax.numpy as jnp
from jax import lax
from jax.experimental import pallas as pl
from jax.experimental.pallas import tpu as pltpu
from jax.sharding import PartitionSpec as P

HD = 128
GUIDANCE = 5.0
SCALE = HD ** (-0.5)
VMEM = 56 * 1024 * 1024
LAST = (((1,), (1,)), ((), ()))
FIRST = (((0,), (0,)), ((), ()))
F32 = jnp.float32
BF16 = jnp.bfloat16


def lasts(us):
    return pl.CostEstimate(flops=1000, bytes_accessed=int(us * 3.69e6), transcendentals=0)


def dot(a, b, dims=(((1,), (0,)), ((), ()))):
    return lax.dot_general(a, b, dims, preferred_element_type=F32)


def params():
    return pltpu.CompilerParams(vmem_limit_bytes=VMEM)


def forward_kernel(q_ref, k_ref, v_ref, p_ref, o_ref):
    rows = o_ref.shape[2]
    for part in range(o_ref.shape[1]):
        at = pl.ds(part * rows, rows)
        scores = dot(q_ref[at, :], k_ref[...], LAST) * SCALE
        exps = jnp.exp(scores - jnp.max(scores, axis=1, keepdims=True))
        probs = (exps / jnp.sum(exps, axis=1, keepdims=True)).astype(BF16)
        p_ref[0, at, :] = probs
        out = dot(probs, v_ref[...]).astype(BF16)
        o_ref[0, part] = out
        o_ref[1, part] = out


def attention_forward(query, key, value, parts):
    seq, width = query.shape
    heads = width // HD
    block = pl.BlockSpec((seq, HD), lambda h: (0, h))
    return pl.pallas_call(
        forward_kernel,
        grid=(heads,),
        in_specs=[block] * 3,
        out_specs=[
            pl.BlockSpec((1, seq, seq), lambda h: (h, 0, 0)),
            pl.BlockSpec((2, parts, seq // parts, HD), lambda h: (0, 0, 0, h)),
        ],
        out_shape=[
            jax.ShapeDtypeStruct((heads, seq, seq), BF16),
            jax.ShapeDtypeStruct((2, parts, seq // parts, width), BF16),
        ],
        compiler_params=params(),
        cost_estimate=lasts(16),
    )(query, key, value)


def backward_kernel(u_ref, p_ref, q_ref, k_ref, v_ref, o_ref, *refs):
    (*g_refs, dq_ref, dk_ref, dv_ref, g_scr, d_scr) = refs
    parts = len(g_refs) - 1
    rows = g_refs[0].shape[0]
    for ahead in range(parts):
        part = lax.rem(u_ref[0] + (parts - ahead), parts)
        at = pl.ds(pl.multiple_of(part * rows, rows), rows)
        block = g_refs[ahead][...]
        if ahead == 0:
            block = (block.astype(F32) + g_refs[parts][...].astype(F32)).astype(BF16)
        g_scr[at, :] = block
        d_scr[at, :] = jnp.sum(
            block.astype(F32) * o_ref[0, part].astype(F32), axis=1, keepdims=True
        )
    probs = p_ref[0]
    grad = g_scr[...]
    grad_probs = dot(grad, v_ref[...], LAST)
    grad_scores = (probs.astype(F32) * (grad_probs - d_scr[...])).astype(BF16)
    dv_ref[...] = dot(probs, grad, FIRST).astype(BF16)
    dq_ref[...] = (dot(grad_scores, k_ref[...]) * SCALE).astype(BF16)
    dk_ref[...] = (dot(grad_scores, q_ref[...], FIRST) * SCALE).astype(BF16)


def attention_backward(place, probs, query, key, value, out, grads):
    seq, width = query.shape
    heads = width // HD
    parts = out.shape[1]
    block = pl.BlockSpec((seq, HD), lambda h, u: (0, h))
    return pl.pallas_call(
        backward_kernel,
        grid_spec=pltpu.PrefetchScalarGridSpec(
            num_scalar_prefetch=1,
            grid=(heads,),
            in_specs=[
                pl.BlockSpec((1, seq, seq), lambda h, u: (h, 0, 0)),
                block,
                block,
                block,
                pl.BlockSpec((1, parts, seq // parts, HD), lambda h, u: (0, 0, 0, h)),
            ]
            + [pl.BlockSpec((seq // parts, HD), lambda h, u: (0, h))] * (parts + 1),
            out_specs=[block] * 3,
            scratch_shapes=[pltpu.VMEM((seq, HD), BF16), pltpu.VMEM((seq, 1), F32)],
        ),
        out_shape=[jax.ShapeDtypeStruct((seq, width), BF16)] * 3,
        compiler_params=params(),
        cost_estimate=lasts(400),
    )(place, probs, query, key, value, out, *grads)


def weight_rows(w_ref):
    blocks = []
    for z in range(0, w_ref.shape[0], 4):
        blocks += [w_ref[z], w_ref[z + 2], w_ref[z + 1], w_ref[z + 3]]
    return jnp.concatenate(blocks, axis=0)


def velocity_kernel(
    b_ref, x_ref, m_ref, w_ref, hown_ref, hoth_ref, hlate_ref, r_ref, up_ref, v_ref, sum_ref, s_scr
):
    step = pl.program_id(0)
    tokens = hown_ref.shape[0]

    @pl.when(step == 0)
    def _():
        s_scr[...] = jnp.zeros_like(s_scr)

    first = b_ref[0] == 0
    own = hown_ref[...].astype(F32)
    oth = jnp.concatenate([hoth_ref[...], hlate_ref[...]], axis=0).astype(F32)
    acc = dot(x_ref[...], weight_rows(w_ref)) + dot(m_ref[...], up_ref[...])
    cond = (jnp.where(first, own, oth) + acc[:tokens]).astype(BF16)
    uncond = (jnp.where(first, oth, own) + acc[tokens:]).astype(BF16)
    v_ref[0] = cond
    v_ref[1] = uncond
    c32, u32, r32 = cond.astype(F32), uncond.astype(F32), r_ref[...].astype(F32)
    for row, term in enumerate((c32 * u32, u32 * u32, r32 * u32)):
        s_scr[pl.ds(row, 1), :] += jnp.sum(term, axis=0, keepdims=True)

    @pl.when(step == pl.num_programs(0) - 1)
    def _():
        totals = jnp.sum(s_scr[...], axis=1, keepdims=True)
        lane = lax.broadcasted_iota(jnp.int32, sum_ref.shape, 1)
        sum_ref[...] = jnp.where(
            lane == 0, totals[0:1], jnp.where(lane == 1, totals[1:2], totals[2:3])
        )


def velocity(branch, attended, middle, weight, hidden, hidden_other, reward, up, copies):
    half = weight.shape[2]
    tokens = hidden.shape[0]
    blocks, block_rows, _ = weight.shape
    depth, rank = blocks * block_rows, up.shape[0]
    tile = 512
    steps = half // tile
    mine = lambda j, b: (0, b[0] * steps + j)
    return pl.pallas_call(
        velocity_kernel,
        grid_spec=pltpu.PrefetchScalarGridSpec(
            num_scalar_prefetch=1,
            grid=(steps,),
            in_specs=[
                pl.BlockSpec((2 * tokens, depth), lambda j, b: (0, 0)),
                pl.BlockSpec((2 * tokens, rank), lambda j, b: (0, 0)),
                pl.BlockSpec((blocks, block_rows, tile), lambda j, b: (0, 0, j)),
                pl.BlockSpec((tokens, tile), mine),
                pl.BlockSpec((hidden_other[0].shape[0], tile), lambda j, b: (0, j)),
                pl.BlockSpec((hidden_other[1].shape[0], tile), lambda j, b: (0, j)),
                pl.BlockSpec((tokens, tile), mine),
                pl.BlockSpec((rank, tile), mine),
            ],
            out_specs=[
                pl.BlockSpec((2, tokens, tile), lambda j, b: (0, 0, j)),
                pl.BlockSpec((8 * copies, 128), lambda j, b: (0, 0)),
            ],
            scratch_shapes=[pltpu.VMEM((8, tile), F32)],
        ),
        out_shape=[
            jax.ShapeDtypeStruct((2, tokens, half), BF16),
            jax.ShapeDtypeStruct((8 * copies, 128), F32),
        ],
        compiler_params=params(),
        cost_estimate=lasts(14),
    )(branch, attended, middle, weight, hidden, *hidden_other, reward, up)


def guidance_kernel(
    b_ref, v_ref, r_ref, sum_ref, own_ref, oth_ref, *cut_refs
):
    totals = sum_ref[0:1, :]
    for at in range(8, sum_ref.shape[0], 8):
        totals = totals + sum_ref[at : at + 1, :]
    inner, energy, pull = totals[:, 0:1], totals[:, 1:2] + 1e-08, totals[:, 2:3]
    scale = inner / energy
    slope = (1.0 - GUIDANCE) * pull / energy
    first = b_ref[0] == 0
    target = r_ref[...].astype(F32)
    cond = v_ref[0].astype(F32)
    uncond = v_ref[1].astype(F32)
    grad0 = GUIDANCE * target + slope * uncond
    grad1 = (
        ((1.0 - GUIDANCE) * scale) * target
        + slope * cond
        + (-2.0 * slope * scale) * uncond
    )
    own_ref[...] = jnp.where(first, grad0, grad1).astype(BF16)
    other = jnp.where(first, grad1, grad0).astype(BF16)
    oth_ref[...] = other
    at = 0
    for cut_ref in cut_refs:
        cut_ref[...] = other[at : at + cut_ref.shape[0]]
        at += cut_ref.shape[0]


def guidance(branch, vel, reward, sums, cuts):
    _, tokens, half = vel.shape
    tile = 640
    steps = half // tile
    mine = lambda j, b: (0, b[0] * steps + j)
    here = lambda j, b: (0, j)
    return pl.pallas_call(
        guidance_kernel,
        grid_spec=pltpu.PrefetchScalarGridSpec(
            num_scalar_prefetch=1,
            grid=(steps,),
            in_specs=[
                pl.BlockSpec((2, tokens, tile), lambda j, b: (0, 0, j)),
                pl.BlockSpec((tokens, tile), mine),
                pl.BlockSpec(sums.shape, lambda j, b: (0, 0)),
            ],
            out_specs=[
                pl.BlockSpec((tokens, tile), mine),
                pl.BlockSpec((tokens, tile), here),
            ]
            + [pl.BlockSpec((cut, tile), here) for cut in cuts],
        ),
        out_shape=[
            jax.ShapeDtypeStruct((tokens, 2 * half), BF16),
            jax.ShapeDtypeStruct((tokens, half), BF16),
        ]
        + [jax.ShapeDtypeStruct((cut, half), BF16) for cut in cuts],
        compiler_params=params(),
        cost_estimate=lasts(4),
    )(branch, vel, reward, sums)


def adapter_part_kernel(b_ref, own_ref, oth_ref, x_ref, m_ref, up_ref, mid_ref, both_ref, m_scr):
    step = pl.program_id(0)
    tokens, tile = own_ref.shape
    groups = both_ref.shape[0] // 2
    up = up_ref[...]
    own, oth = own_ref[...], oth_ref[...]
    part = dot(jnp.concatenate([own, oth], axis=0), up, LAST)
    own_at = pl.ds(pl.multiple_of(b_ref[0] * tokens, tokens), tokens)
    oth_at = pl.ds(pl.multiple_of((1 - b_ref[0]) * tokens, tokens), tokens)
    up_part = dot(m_ref[own_at, :], own, FIRST) + dot(m_ref[oth_at, :], oth, FIRST)
    up_part = up_part.astype(BF16)
    for row in range(groups):
        both_ref[groups + row, step] = up_part[16 * row : 16 * row + 16]

    @pl.when(step == 0)
    def _():
        m_scr[...] = part

    @pl.when(step > 0)
    def _():
        m_scr[...] += part

    @pl.when(step == pl.num_programs(0) - 1)
    def _():
        mid = m_scr[...].astype(BF16)
        mid_ref[...] = mid
        down_part = dot(mid[:tokens], x_ref[own_at, :], FIRST)
        down_part = (down_part + dot(mid[tokens:], x_ref[oth_at, :], FIRST)).astype(BF16)
        for row in range(groups):
            for lane in range(both_ref.shape[1]):
                both_ref[row, lane] = down_part[
                    16 * row : 16 * row + 16, lane * tile : lane * tile + tile
                ]


def adapter_part(branch, grad_own, grad_other, attended, middle, up):
    tokens, half = grad_other.shape
    rank, depth = up.shape[0], attended.shape[1]
    tile = 640
    steps = half // tile
    whole = lambda j, b: (0, 0)
    mine = lambda j, b: (0, b[0] * steps + j)
    both = (2 * rank // 16, steps, 16, tile)
    return pl.pallas_call(
        adapter_part_kernel,
        grid_spec=pltpu.PrefetchScalarGridSpec(
            num_scalar_prefetch=1,
            grid=(steps,),
            in_specs=[
                pl.BlockSpec((tokens, tile), mine),
                pl.BlockSpec((tokens, tile), lambda j, b: (0, j)),
                pl.BlockSpec((2 * tokens, depth), whole),
                pl.BlockSpec((2 * tokens, rank), whole),
                pl.BlockSpec((rank, tile), mine),
            ],
            out_specs=[
                pl.BlockSpec((2 * tokens, rank), whole),
                pl.BlockSpec(both, lambda j, b: (0, 0, 0, 0)),
            ],
            scratch_shapes=[pltpu.VMEM((2 * tokens, rank), F32)],
        ),
        out_shape=[
            jax.ShapeDtypeStruct((2 * tokens, rank), BF16),
            jax.ShapeDtypeStruct(both, BF16),
        ],
        compiler_params=params(),
        cost_estimate=lasts(5),
    )(branch, grad_own, grad_other, attended, middle, up)


def gradient_kernel(u_ref, b_ref, own_ref, oth_ref, mid_ref, w_ref, down_ref, *refs):
    step = pl.program_id(0)
    tokens = own_ref.shape[0]
    rows = jnp.concatenate([own_ref[...], oth_ref[...]], axis=0)
    part = dot(rows, weight_rows(w_ref), LAST) + dot(mid_ref[...], down_ref[...])
    part = part.astype(BF16)
    *gown_refs, first_ref, rest_ref, near_ref = refs
    last = len(gown_refs) - 1
    for at in range(last + 1):

        @pl.when(step == at)
        def _():
            gown_refs[at][...] = part[:tokens]
            if at == 0:
                first_ref[...] = part[tokens:]
            elif at < last:
                rest_ref[(at - 1) * tokens : at * tokens] = part[tokens:]
            else:
                near_ref[...] = part[tokens:]


def gradient(place, branch, grad_own, grad_other, grad_middle, weight, down_rows, parts):
    tokens, half = grad_other.shape
    blocks, block_rows, _ = weight.shape
    rank, depth = down_rows.shape
    wide = depth // parts
    whole = lambda j, u, b: (0, 0)
    there = lambda j, u: lax.rem(u[0] + 1 + j, parts)
    return pl.pallas_call(
        gradient_kernel,
        grid_spec=pltpu.PrefetchScalarGridSpec(
            num_scalar_prefetch=2,
            grid=(parts,),
            in_specs=[
                pl.BlockSpec((tokens, half), lambda j, u, b: (0, b[0])),
                pl.BlockSpec((tokens, half), whole),
                pl.BlockSpec((2 * tokens, rank), whole),
                pl.BlockSpec(
                    (blocks // parts, block_rows, half), lambda j, u, b: (there(j, u), 0, 0)
                ),
                pl.BlockSpec((rank, wide), lambda j, u, b: (0, there(j, u))),
            ],
            out_specs=[pl.BlockSpec((tokens, wide), whole)] * parts
            + [
                pl.BlockSpec((tokens, wide), whole),
                pl.BlockSpec(((parts - 2) * tokens, wide), whole),
                pl.BlockSpec((tokens, wide), whole),
            ],
        ),
        out_shape=[jax.ShapeDtypeStruct((tokens, wide), BF16)] * parts
        + [
            jax.ShapeDtypeStruct((tokens, wide), BF16),
            jax.ShapeDtypeStruct(((parts - 2) * tokens, wide), BF16),
            jax.ShapeDtypeStruct((tokens, wide), BF16),
        ],
        compiler_params=params(),
        cost_estimate=lasts(14),
    )(place, branch, grad_own, grad_other, grad_middle, weight, down_rows)


def adapter_kernel(p_ref, down_ref, up_ref):
    members, parts, _, rows, tile = p_ref.shape
    half = down_ref.shape[1]
    lanes = half // tile
    groups = parts * members // lanes
    for u in range(parts):
        for c in range(members):
            row, lane = divmod(u * members + c, lanes)
            columns = pl.ds(lane * tile, tile)
            if row < groups // 2:
                both = p_ref[c, u, 0].astype(F32) + p_ref[c, u, 1].astype(F32)
                down_ref[pl.ds(row * rows, rows), columns] = both
            else:
                at = pl.ds((row - groups // 2) * rows, rows)
                for b in range(2):
                    up_ref[at, pl.ds(b * half + lane * tile, tile)] = p_ref[c, u, b].astype(F32)


def adapter(pieces, rank, lanes):
    half = lanes * pieces.shape[4]
    return pl.pallas_call(
        adapter_kernel,
        out_shape=[
            jax.ShapeDtypeStruct((rank, half), F32),
            jax.ShapeDtypeStruct((rank, 2 * half), F32),
        ],
        in_specs=[pl.BlockSpec(memory_space=pltpu.VMEM)],
        out_specs=[pl.BlockSpec(memory_space=pltpu.VMEM)] * 2,
        compiler_params=params(),
        cost_estimate=lasts(3),
    )(pieces)


def exchange(block, axes):
    return lax.all_to_all(block, axes, split_axis=0, concat_axis=0, tiled=True)


def swap(block):
    return lax.ppermute(block, "branch", [(0, 1), (1, 0)])


def ahead_send(block, ahead):
    parts = lax.axis_size("ulysses")
    return lax.ppermute(block, "ulysses", [(u, (u + ahead) % parts) for u in range(parts)])


def send_x(block, step):
    clips = lax.axis_size("fsdp")
    route = []
    for at in range(2 * clips):
        b, f = divmod(at, clips)
        z, rest = divmod(f, 4)
        near, core = divmod(rest, 2)
        x = (b * 2 + near + step) % 4
        route.append((at, (x // 2) * clips + z * 4 + (x % 2) * 2 + core))
    return lax.ppermute(block, ("branch", "fsdp"), route)


def gather_operand(rows, branch, half):
    near = lax.rem(lax.axis_index("fsdp") // 2, 2)
    top = rows.shape[0] // 2
    columns = lambda part, b: lax.dynamic_slice_in_dim(part, b * half, half, 1)
    forward = jnp.where(near == 0, branch, 1 - branch)
    before = send_x(columns(rows[:top], forward), 1)
    after = send_x(columns(rows[top:], 1 - forward), -1)
    beside = jnp.concatenate([before, after], axis=0)
    mine = columns(rows, branch)
    return jnp.where(
        near == 0,
        jnp.concatenate([mine, beside], axis=0),
        jnp.concatenate([beside, mine], axis=0),
    )


def body(
    hidden,
    query,
    key,
    value,
    output_projection_weight,
    adapter_down_weight,
    adapter_up_weight,
    reward_gradient,
):
    parts = lax.axis_size("ulysses")
    clips = lax.axis_size("fsdp")
    branch = lax.axis_index("branch")
    branch_word = branch.reshape(1).astype(jnp.int32)
    place = lax.axis_index("ulysses").reshape(1).astype(jnp.int32)
    _, _, tokens, model = hidden.shape
    half = model // 2
    _, _, seq, width = query.shape
    depth, rank = adapter_down_weight.shape
    query2, key2, value2 = (a.reshape(seq, width) for a in (query, key, value))
    hidden2 = hidden.reshape(tokens, model)
    reward2 = reward_gradient.reshape(tokens, model)

    operand = gather_operand(output_projection_weight, branch, half)
    operand, query2, hidden_ready = lax.optimization_barrier((operand, query2, hidden2))
    weight_groups = [
        [z * 4 + near * 2 + core for z in range(clips // 4) for core in (0, 1)] for near in (0, 1)
    ]
    weight = lax.all_gather(operand, "fsdp", axis=0, tiled=True, axis_index_groups=weight_groups)
    weight = weight.reshape(clips, depth // clips, half)
    hidden_send = lax.dynamic_slice_in_dim(hidden_ready, (1 - branch) * half, half, 1)
    early = 5 * tokens // 8
    hidden_early = swap(hidden_send[:early])

    probs, attended = attention_forward(query2, key2, value2, parts)
    attended, hidden_early = lax.optimization_barrier((attended, hidden_early))
    gathered = exchange(attended.reshape(2 * seq, width), ("branch", "ulysses"))
    gathered, hidden_send = lax.optimization_barrier((gathered, hidden_send))
    hidden_late = swap(hidden_send[early:])
    gathered = gathered.reshape(2, parts, tokens, width).transpose(0, 2, 1, 3)
    gathered = gathered.reshape(2 * tokens, depth)
    middle = dot(gathered, adapter_down_weight).astype(BF16)

    vel, sums = velocity(
        branch_word, gathered, middle, weight, hidden2, (hidden_early, hidden_late), reward2,
        adapter_up_weight, 2 * parts,
    )
    sums = exchange(sums, ("branch", "ulysses"))
    cuts = (3 * tokens // 8, 7 * tokens // 16, 3 * tokens // 16)
    grad_hidden, grad_other, *pieces_out = guidance(branch_word, vel, reward2, sums, cuts)
    received = [swap(pieces_out[0])]
    grad_middle, both = adapter_part(
        branch_word, grad_hidden, grad_other, gathered, middle, adapter_up_weight
    )

    groups = [
        [u * clips + z * 4 + near * 2 + core for u in range(parts) for z in range(clips // 4) for core in (0, 1)]
        for near in (0, 1)
    ]
    spread = lambda block: lax.all_to_all(
        block, ("ulysses", "fsdp"), split_axis=0, concat_axis=0, tiled=True, axis_index_groups=groups
    )
    row_groups, lanes, rows, tile = both.shape
    pieces = row_groups * lanes
    both = spread(both.reshape(pieces * rows, tile))
    grad_other, pieces_out[1], received[0] = lax.optimization_barrier(
        (grad_other, pieces_out[1], received[0])
    )
    received.append(swap(pieces_out[1]))

    down_rows = adapter_down_weight.T
    *grads, far_first, far, close = gradient(
        place, branch_word, grad_hidden, grad_other, grad_middle, weight, down_rows, parts
    )
    both, pieces_out[2], received[1], grads[3] = lax.optimization_barrier(
        (both.reshape(pieces, rows, tile), pieces_out[2], received[1], grads[3])
    )
    far_first = swap(far_first)
    total = jnp.sum(both.astype(F32), axis=0)
    beside = [send_x(total, step) for step in (1, 2, 3)]
    far, far_first, *beside = lax.optimization_barrier((far, far_first, *beside))
    far = swap(far)
    far, close = lax.optimization_barrier((far, close))
    close = swap(close)
    far = far.reshape(parts - 2, tokens, width)
    halves = [far_first] + [far[at] for at in range(parts - 2)]
    routed = [
        ahead_send((grads[at].astype(F32) + block.astype(F32)).astype(BF16), at + 1)
        for at, block in enumerate(halves)
    ]
    close, pieces_out[2] = lax.optimization_barrier((close, pieces_out[2]))
    received.append(swap(pieces_out[2]))
    near = lax.rem(lax.axis_index("fsdp") // 2, 2)
    own_total = total + jnp.where(near == 0, beside[2], beside[0])
    other_total = beside[1] + jnp.where(near == 0, beside[0], beside[2])
    total = jnp.where(
        branch == 0,
        jnp.concatenate([own_total, other_total]),
        jnp.concatenate([other_total, own_total]),
    ).astype(BF16)
    ring = [total] + [ahead_send(total, ahead) for ahead in range(1, parts)]
    ring = jnp.concatenate(ring[::-1] * 2, axis=0)
    column = lax.dynamic_slice_in_dim(
        ring, (parts - 1 - place[0]) * 2 * rows, parts * 2 * rows, 0
    )
    grads = [grads[parts - 1]] + routed + [close]
    packed = lax.all_gather(column, "fsdp", axis=0, tiled=True, axis_index_groups=weight_groups)
    down_gradient_rows, adapter_up_gradient = adapter(
        packed.reshape(clips // 2, parts, 2, rows, tile), rank, lanes
    )

    grad_query, grad_key, grad_value = attention_backward(
        place, probs, query2, key2, value2, attended, grads
    )
    received = jnp.concatenate(received, axis=0)
    grad_hidden = lax.dynamic_update_slice_in_dim(grad_hidden, received, (1 - branch) * half, 1)
    return (
        grad_hidden.reshape(hidden.shape),
        grad_query.reshape(query.shape),
        grad_key.reshape(key.shape),
        grad_value.reshape(value.shape),
        down_gradient_rows.T,
        adapter_up_gradient,
    )


def solution(mesh):
    in_specs = (
        P("branch", "fsdp", "ulysses", None),
        P("branch", "fsdp", None, "ulysses"),
        P("branch", "fsdp", None, "ulysses"),
        P("branch", "fsdp", None, "ulysses"),
        P("fsdp", None),
        P(),
        P(),
        P("fsdp", "ulysses", None),
    )
    out_specs = (
        P("branch", "fsdp", "ulysses", None),
        P("branch", "fsdp", None, "ulysses"),
        P("branch", "fsdp", None, "ulysses"),
        P("branch", "fsdp", None, "ulysses"),
        P(),
        P(),
    )
    return jax.shard_map(body, mesh=mesh, in_specs=in_specs, out_specs=out_specs, check_vma=False)
```

```python
import functools

import jax
import jax.numpy as jnp
from jax import lax
from jax.experimental import pallas as pl
from jax.experimental.pallas import tpu as pltpu
from jax.sharding import PartitionSpec as P

HD = 128
GUIDANCE = 5.0
SCALE = HD ** (-0.5)
VMEM = 56 * 1024 * 1024
LAST = (((1,), (1,)), ((), ()))
FIRST = (((0,), (0,)), ((), ()))
F32 = jnp.float32
BF16 = jnp.bfloat16


def lasts(us):
    return pl.CostEstimate(flops=1000, bytes_accessed=int(us * 3.69e6), transcendentals=0)


def dot(a, b, dims=(((1,), (0,)), ((), ()))):
    return lax.dot_general(a, b, dims, preferred_element_type=F32)


def params():
    return pltpu.CompilerParams(vmem_limit_bytes=VMEM)


def forward_kernel(q_ref, k_ref, v_ref, p_ref, o_ref):
    rows = o_ref.shape[2]
    for part in range(o_ref.shape[1]):
        at = pl.ds(part * rows, rows)
        scores = dot(k_ref[...], q_ref[at, :], LAST) * SCALE
        exps = jnp.exp(scores - jnp.max(scores, axis=0, keepdims=True))
        probs = (exps * (1.0 / jnp.sum(exps, axis=0, keepdims=True))).astype(BF16)
        p_ref[0, :, at] = probs
        out = dot(probs, v_ref[...], FIRST).astype(BF16)
        o_ref[0, part] = out
        o_ref[1, part] = out


def attention_forward(query, key, value, parts):
    seq, width = query.shape
    heads = width // HD
    block = pl.BlockSpec((seq, HD), lambda h: (0, h))
    return pl.pallas_call(
        forward_kernel,
        grid=(heads,),
        in_specs=[block] * 3,
        out_specs=[
            pl.BlockSpec((1, seq, seq), lambda h: (h, 0, 0)),
            pl.BlockSpec((2, parts, seq // parts, HD), lambda h: (0, 0, 0, h)),
        ],
        out_shape=[
            jax.ShapeDtypeStruct((heads, seq, seq), BF16),
            jax.ShapeDtypeStruct((2, parts, seq // parts, width), BF16),
        ],
        compiler_params=params(),
        cost_estimate=lasts(16),
    )(query, key, value)


def backward_kernel(u_ref, p_ref, q_ref, k_ref, v_ref, o_ref, *refs):
    (*g_refs, dq_ref, dk_ref, dv_ref, g_scr) = refs
    parts = len(g_refs) - 1
    rows, size = g_refs[0].shape
    for ahead in range(parts):
        part = lax.rem(u_ref[0] + (parts - ahead), parts)
        block = g_refs[ahead][...]
        if ahead == 0:
            block = (block.astype(F32) + g_refs[parts][...].astype(F32)).astype(BF16)
        g_scr[pl.ds(pl.multiple_of(part * rows, rows), rows), :] = block
    probs = p_ref[0]
    grad = g_scr[...]
    out = o_ref[0].reshape(parts * rows, size)
    delta = jnp.sum((grad.astype(F32) * out.astype(F32)).T, axis=0, keepdims=True)
    grad_probs = dot(v_ref[...], grad, LAST)
    grad_scores = (probs.astype(F32) * (grad_probs - delta)).astype(BF16)
    dv_ref[...] = dot(probs, grad).astype(BF16)
    dk_ref[...] = (dot(grad_scores, q_ref[...]) * SCALE).astype(BF16)
    dq_ref[...] = (dot(k_ref[...].T, grad_scores) * SCALE).T.astype(BF16)


def attention_backward(place, probs, query, key, value, out, grads):
    seq, width = query.shape
    heads = width // HD
    parts = out.shape[1]
    block = pl.BlockSpec((seq, HD), lambda h, u: (0, h))
    return pl.pallas_call(
        backward_kernel,
        grid_spec=pltpu.PrefetchScalarGridSpec(
            num_scalar_prefetch=1,
            grid=(heads,),
            in_specs=[
                pl.BlockSpec((1, seq, seq), lambda h, u: (h, 0, 0)),
                block,
                block,
                block,
                pl.BlockSpec((1, parts, seq // parts, HD), lambda h, u: (0, 0, 0, h)),
            ]
            + [pl.BlockSpec((seq // parts, HD), lambda h, u: (0, h))] * (parts + 1),
            out_specs=[block] * 3,
            scratch_shapes=[pltpu.VMEM((seq, HD), BF16)],
        ),
        out_shape=[jax.ShapeDtypeStruct((seq, width), BF16)] * 3,
        compiler_params=params(),
        cost_estimate=lasts(400),
    )(place, probs, query, key, value, out, *grads)


def weight_rows(w_ref):
    blocks = []
    for z in range(0, w_ref.shape[0], 4):
        blocks += [w_ref[z], w_ref[z + 2], w_ref[z + 1], w_ref[z + 3]]
    return jnp.concatenate(blocks, axis=0)


def velocity_kernel(
    b_ref, x_ref, m_ref, w_ref, hown_ref, hoth_ref, hlate_ref, r_ref, up_ref, v_ref, sum_ref, s_scr
):
    step = pl.program_id(0)
    tokens = hown_ref.shape[0]

    @pl.when(step == 0)
    def _():
        s_scr[...] = jnp.zeros_like(s_scr)

    first = b_ref[0] == 0
    own = hown_ref[...].astype(F32)
    oth = jnp.concatenate([hoth_ref[...], hlate_ref[...]], axis=0).astype(F32)
    acc = dot(x_ref[...], weight_rows(w_ref)) + dot(m_ref[...], up_ref[...])
    cond = (jnp.where(first, own, oth) + acc[:tokens]).astype(BF16)
    uncond = (jnp.where(first, oth, own) + acc[tokens:]).astype(BF16)
    v_ref[0] = cond
    v_ref[1] = uncond
    c32, u32, r32 = cond.astype(F32), uncond.astype(F32), r_ref[...].astype(F32)
    for row, term in enumerate((c32 * u32, u32 * u32, r32 * u32)):
        s_scr[pl.ds(row, 1), :] += jnp.sum(term, axis=0, keepdims=True)

    @pl.when(step == pl.num_programs(0) - 1)
    def _():
        totals = jnp.sum(s_scr[...], axis=1, keepdims=True)
        lane = lax.broadcasted_iota(jnp.int32, sum_ref.shape, 1)
        sum_ref[...] = jnp.where(
            lane == 0, totals[0:1], jnp.where(lane == 1, totals[1:2], totals[2:3])
        )


def velocity(branch, attended, middle, weight, hidden, hidden_other, reward, up, copies):
    half = weight.shape[2]
    tokens = hidden.shape[0]
    blocks, block_rows, _ = weight.shape
    depth, rank = blocks * block_rows, up.shape[0]
    tile = 512
    steps = half // tile
    mine = lambda j, b: (0, b[0] * steps + j)
    return pl.pallas_call(
        velocity_kernel,
        grid_spec=pltpu.PrefetchScalarGridSpec(
            num_scalar_prefetch=1,
            grid=(steps,),
            in_specs=[
                pl.BlockSpec((2 * tokens, depth), lambda j, b: (0, 0)),
                pl.BlockSpec((2 * tokens, rank), lambda j, b: (0, 0)),
                pl.BlockSpec((blocks, block_rows, tile), lambda j, b: (0, 0, j)),
                pl.BlockSpec((tokens, tile), mine),
                pl.BlockSpec((hidden_other[0].shape[0], tile), lambda j, b: (0, j)),
                pl.BlockSpec((hidden_other[1].shape[0], tile), lambda j, b: (0, j)),
                pl.BlockSpec((tokens, tile), mine),
                pl.BlockSpec((rank, tile), mine),
            ],
            out_specs=[
                pl.BlockSpec((2, tokens, tile), lambda j, b: (0, 0, j)),
                pl.BlockSpec((8 * copies, 128), lambda j, b: (0, 0)),
            ],
            scratch_shapes=[pltpu.VMEM((8, tile), F32)],
        ),
        out_shape=[
            jax.ShapeDtypeStruct((2, tokens, half), BF16),
            jax.ShapeDtypeStruct((8 * copies, 128), F32),
        ],
        compiler_params=params(),
        cost_estimate=lasts(14),
    )(branch, attended, middle, weight, hidden, *hidden_other, reward, up)


def guidance_kernel(
    b_ref, v_ref, r_ref, sum_ref, x_ref, m_ref, up_ref,
    own_ref, oth_ref, mid_ref, both_ref, *refs,
):
    step = pl.program_id(0)
    tokens, tile = r_ref.shape
    (*cut_refs, m_scr) = refs
    groups = both_ref.shape[0] // 2
    totals = sum_ref[0:1, :]
    for at in range(8, sum_ref.shape[0], 8):
        totals = totals + sum_ref[at : at + 1, :]
    inner, energy, pull = totals[:, 0:1], totals[:, 1:2] + 1e-08, totals[:, 2:3]
    scale = inner / energy
    slope = (1.0 - GUIDANCE) * pull / energy
    first = b_ref[0] == 0
    target = r_ref[...].astype(F32)
    cond = v_ref[0].astype(F32)
    uncond = v_ref[1].astype(F32)
    grad0 = (GUIDANCE * target + slope * uncond).astype(BF16)
    grad1 = (
        ((1.0 - GUIDANCE) * scale) * target
        + slope * cond
        + (-2.0 * slope * scale) * uncond
    ).astype(BF16)
    own_ref[...] = jnp.where(first, grad0, grad1)
    other = jnp.where(first, grad1, grad0)
    oth_ref[...] = other
    at = 0
    for cut_ref in cut_refs:
        cut_ref[...] = other[at : at + cut_ref.shape[0]]
        at += cut_ref.shape[0]
    up = up_ref[...]
    part = jnp.concatenate([dot(grad0, up, LAST), dot(grad1, up, LAST)], axis=0)
    up_part = dot(m_ref[:tokens], grad0, FIRST) + dot(m_ref[tokens:], grad1, FIRST)
    up_part = up_part.astype(BF16)
    for row in range(groups):
        both_ref[groups + row, step] = up_part[16 * row : 16 * row + 16]

    @pl.when(step == 0)
    def _():
        m_scr[...] = part

    @pl.when(step > 0)
    def _():
        m_scr[...] += part

    @pl.when(step == pl.num_programs(0) - 1)
    def _():
        mid = m_scr[...].astype(BF16)
        mid_ref[0:tokens] = jnp.where(first, mid[:tokens], mid[tokens:])
        mid_ref[tokens:] = jnp.where(first, mid[tokens:], mid[:tokens])
        down_part = dot(mid, x_ref[...], FIRST).astype(BF16)
        for row in range(groups):
            for lane in range(both_ref.shape[1]):
                both_ref[row, lane] = down_part[
                    16 * row : 16 * row + 16, lane * tile : lane * tile + tile
                ]


def guidance(branch, vel, reward, sums, attended, middle, up, cuts):
    _, tokens, half = vel.shape
    rank, depth = up.shape[0], attended.shape[1]
    tile = 640
    steps = half // tile
    whole = lambda j, b: (0, 0)
    mine = lambda j, b: (0, b[0] * steps + j)
    here = lambda j, b: (0, j)
    both = (2 * rank // 16, steps, 16, tile)
    return pl.pallas_call(
        guidance_kernel,
        grid_spec=pltpu.PrefetchScalarGridSpec(
            num_scalar_prefetch=1,
            grid=(steps,),
            in_specs=[
                pl.BlockSpec((2, tokens, tile), lambda j, b: (0, 0, j)),
                pl.BlockSpec((tokens, tile), mine),
                pl.BlockSpec(sums.shape, whole),
                pl.BlockSpec((2 * tokens, depth), whole),
                pl.BlockSpec((2 * tokens, rank), whole),
                pl.BlockSpec((rank, tile), mine),
            ],
            out_specs=[
                pl.BlockSpec((tokens, tile), mine),
                pl.BlockSpec((tokens, tile), here),
                pl.BlockSpec((2 * tokens, rank), whole),
                pl.BlockSpec(both, lambda j, b: (0, 0, 0, 0)),
            ]
            + [pl.BlockSpec((cut, tile), here) for cut in cuts],
            scratch_shapes=[pltpu.VMEM((2 * tokens, rank), F32)],
        ),
        out_shape=[
            jax.ShapeDtypeStruct((tokens, 2 * half), BF16),
            jax.ShapeDtypeStruct((tokens, half), BF16),
            jax.ShapeDtypeStruct((2 * tokens, rank), BF16),
            jax.ShapeDtypeStruct(both, BF16),
        ]
        + [jax.ShapeDtypeStruct((cut, half), BF16) for cut in cuts],
        compiler_params=params(),
        cost_estimate=lasts(8),
    )(branch, vel, reward, sums, attended, middle, up)


def gradient_kernel(u_ref, b_ref, own_ref, oth_ref, mid_ref, w_ref, down_ref, *refs):
    step = pl.program_id(0)
    tokens = own_ref.shape[0]
    rows = jnp.concatenate([own_ref[...], oth_ref[...]], axis=0)
    part = dot(rows, weight_rows(w_ref), LAST) + dot(mid_ref[...], down_ref[...])
    part = part.astype(BF16)
    *gown_refs, far_ref, near_ref = refs
    last = len(gown_refs) - 1
    for at in range(last + 1):

        @pl.when(step == at)
        def _():
            gown_refs[at][...] = part[:tokens]
            if at < last:
                far_ref[at * tokens : (at + 1) * tokens] = part[tokens:]
            else:
                near_ref[...] = part[tokens:]


def gradient(place, branch, grad_own, grad_other, grad_middle, weight, down_rows, parts):
    tokens, half = grad_other.shape
    blocks, block_rows, _ = weight.shape
    rank, depth = down_rows.shape
    wide = depth // parts
    whole = lambda j, u, b: (0, 0)
    there = lambda j, u: lax.rem(u[0] + 1 + j, parts)
    return pl.pallas_call(
        gradient_kernel,
        grid_spec=pltpu.PrefetchScalarGridSpec(
            num_scalar_prefetch=2,
            grid=(parts,),
            in_specs=[
                pl.BlockSpec((tokens, half), lambda j, u, b: (0, b[0])),
                pl.BlockSpec((tokens, half), whole),
                pl.BlockSpec((2 * tokens, rank), whole),
                pl.BlockSpec(
                    (blocks // parts, block_rows, half), lambda j, u, b: (there(j, u), 0, 0)
                ),
                pl.BlockSpec((rank, wide), lambda j, u, b: (0, there(j, u))),
            ],
            out_specs=[pl.BlockSpec((tokens, wide), whole)] * parts
            + [
                pl.BlockSpec(((parts - 1) * tokens, wide), whole),
                pl.BlockSpec((tokens, wide), whole),
            ],
        ),
        out_shape=[jax.ShapeDtypeStruct((tokens, wide), BF16)] * parts
        + [
            jax.ShapeDtypeStruct(((parts - 1) * tokens, wide), BF16),
            jax.ShapeDtypeStruct((tokens, wide), BF16),
        ],
        compiler_params=params(),
        cost_estimate=lasts(14),
    )(place, branch, grad_own, grad_other, grad_middle, weight, down_rows)


def adapter_kernel(p_ref, down_ref, up_ref):
    members, _, _, rows, tile = p_ref.shape
    half = down_ref.shape[1]
    lanes = half // tile

    @pl.when(pl.program_id(0) < pl.num_programs(0) // 2)
    def _():
        for c in range(members):
            row, lane = divmod(c, lanes)
            both = p_ref[c, 0, 0].astype(F32) + p_ref[c, 0, 1].astype(F32)
            down_ref[pl.ds(row * rows, rows), pl.ds(lane * tile, tile)] = both

    @pl.when(pl.program_id(0) >= pl.num_programs(0) // 2)
    def _():
        for c in range(members):
            row, lane = divmod(c, lanes)
            for b in range(2):
                columns = pl.ds(b * half + lane * tile, tile)
                up_ref[pl.ds(row * rows, rows), columns] = p_ref[c, 0, b].astype(F32)


def adapter(pieces, rank, lanes):
    members, parts, _, rows, tile = pieces.shape
    half = lanes * tile
    span = members // lanes * rows
    first_up = parts // 2
    return pl.pallas_call(
        adapter_kernel,
        grid=(parts,),
        out_shape=[
            jax.ShapeDtypeStruct((rank, half), F32),
            jax.ShapeDtypeStruct((rank, 2 * half), F32),
        ],
        in_specs=[pl.BlockSpec((members, 1, 2, rows, tile), lambda u: (0, u, 0, 0, 0))],
        out_specs=[
            pl.BlockSpec((span, half), lambda u: (jnp.minimum(u, first_up - 1), 0)),
            pl.BlockSpec((span, 2 * half), lambda u: (jnp.maximum(u - first_up, 0), 0)),
        ],
        compiler_params=params(),
        cost_estimate=lasts(3),
    )(pieces)


def exchange(block, axes):
    return lax.all_to_all(block, axes, split_axis=0, concat_axis=0, tiled=True)


def swap(block):
    return lax.ppermute(block, "branch", [(0, 1), (1, 0)])


def ahead_send(block, ahead):
    parts = lax.axis_size("ulysses")
    return lax.ppermute(block, "ulysses", [(u, (u + ahead) % parts) for u in range(parts)])


def send_x(block, step):
    clips = lax.axis_size("fsdp")
    route = []
    for at in range(2 * clips):
        b, f = divmod(at, clips)
        z, rest = divmod(f, 4)
        near, core = divmod(rest, 2)
        x = (b * 2 + near + step) % 4
        route.append((at, (x // 2) * clips + z * 4 + (x % 2) * 2 + core))
    return lax.ppermute(block, ("branch", "fsdp"), route)


def gather_operand(rows, branch, half):
    near = lax.rem(lax.axis_index("fsdp") // 2, 2)
    top = rows.shape[0] // 2
    columns = lambda part, b: lax.dynamic_slice_in_dim(part, b * half, half, 1)
    forward = jnp.where(near == 0, branch, 1 - branch)
    before = send_x(columns(rows[:top], forward), 1)
    after = send_x(columns(rows[top:], 1 - forward), -1)
    beside = jnp.concatenate([before, after], axis=0)
    mine = columns(rows, branch)
    return jnp.where(
        near == 0,
        jnp.concatenate([mine, beside], axis=0),
        jnp.concatenate([beside, mine], axis=0),
    )


def body(
    hidden,
    query,
    key,
    value,
    output_projection_weight,
    adapter_down_weight,
    adapter_up_weight,
    reward_gradient,
):
    parts = lax.axis_size("ulysses")
    clips = lax.axis_size("fsdp")
    branch = lax.axis_index("branch")
    branch_word = branch.reshape(1).astype(jnp.int32)
    place = lax.axis_index("ulysses").reshape(1).astype(jnp.int32)
    _, _, tokens, model = hidden.shape
    half = model // 2
    _, _, seq, width = query.shape
    depth, rank = adapter_down_weight.shape
    query2, key2, value2 = (a.reshape(seq, width) for a in (query, key, value))
    hidden2 = hidden.reshape(tokens, model)
    reward2 = reward_gradient.reshape(tokens, model)

    operand = gather_operand(output_projection_weight, branch, half)
    operand, query2, hidden_ready = lax.optimization_barrier((operand, query2, hidden2))
    weight_groups = [
        [z * 4 + near * 2 + core for z in range(clips // 4) for core in (0, 1)] for near in (0, 1)
    ]
    weight = lax.all_gather(operand, "fsdp", axis=0, tiled=True, axis_index_groups=weight_groups)
    weight = weight.reshape(clips, depth // clips, half)
    early = 5 * tokens // 8
    hidden_send = lax.dynamic_slice_in_dim(hidden_ready, (1 - branch) * half, half, 1)
    hidden_early = swap(hidden_send[:early])
    hidden_late = hidden_send[early:]

    probs, attended = attention_forward(query2, key2, value2, parts)
    attended, hidden_early = lax.optimization_barrier((attended, hidden_early))
    gathered = exchange(attended.reshape(2 * seq, width), ("branch", "ulysses"))
    gathered, hidden_late = lax.optimization_barrier((gathered, hidden_late))
    hidden_late = swap(hidden_late)
    gathered = gathered.reshape(2, parts, tokens, width).transpose(0, 2, 1, 3)
    gathered = gathered.reshape(2 * tokens, depth)
    middle = dot(gathered, adapter_down_weight).astype(BF16)

    vel, sums = velocity(
        branch_word, gathered, middle, weight, hidden2, (hidden_early, hidden_late), reward2,
        adapter_up_weight, 2 * parts,
    )
    sums = exchange(sums, ("branch", "ulysses"))
    cuts = (tokens // 2, tokens // 2)
    grad_hidden, grad_other, grad_middle, both, *pieces_out = guidance(
        branch_word, vel, reward2, sums, gathered, middle, adapter_up_weight, cuts
    )
    received = [swap(pieces_out[0])]

    groups = [
        [u * clips + z * 4 + near * 2 + core for u in range(parts) for z in range(clips // 4) for core in (0, 1)]
        for near in (0, 1)
    ]
    spread = lambda block: lax.all_to_all(
        block, ("ulysses", "fsdp"), split_axis=0, concat_axis=0, tiled=True, axis_index_groups=groups
    )
    row_groups, lanes, rows, tile = both.shape
    pieces = row_groups * lanes
    down_rows = adapter_down_weight.T
    *grads, far, close = gradient(
        place, branch_word, grad_hidden, grad_other, grad_middle, weight, down_rows, parts
    )
    far = swap(far)
    both, grads[3], received[0] = lax.optimization_barrier((both, grads[3], received[0]))
    both = spread(both.reshape(pieces * rows, tile))
    total = jnp.sum(both.reshape(pieces, rows, tile).astype(F32), axis=0)
    beside = [send_x(total, step) for step in (1, 2, 3)]
    far, close, *beside = lax.optimization_barrier((far, close, *beside))
    close = swap(close)
    far = far.reshape(parts - 1, tokens, width)
    routed = [
        ahead_send((grads[at].astype(F32) + far[at].astype(F32)).astype(BF16), at + 1)
        for at in range(parts - 1)
    ]
    close, pieces_out[1], *routed = lax.optimization_barrier((close, pieces_out[1], *routed))
    received.append(swap(pieces_out[1]))

    near = lax.rem(lax.axis_index("fsdp") // 2, 2)
    own_total = total + jnp.where(near == 0, beside[2], beside[0])
    other_total = beside[1] + jnp.where(near == 0, beside[0], beside[2])
    total = jnp.where(
        branch == 0,
        jnp.concatenate([own_total, other_total]),
        jnp.concatenate([other_total, own_total]),
    ).astype(BF16)
    ring = [total] + [ahead_send(total, ahead) for ahead in range(1, parts)]
    ring = jnp.concatenate(ring[::-1] * 2, axis=0)
    column = lax.dynamic_slice_in_dim(
        ring, (parts - 1 - place[0]) * 2 * rows, parts * 2 * rows, 0
    )
    packed = lax.all_gather(column, "fsdp", axis=0, tiled=True, axis_index_groups=weight_groups)
    packed = packed.reshape(clips // 2, parts, 2, rows, tile)
    down_gradient_rows, adapter_up_gradient = adapter(packed, rank, lanes)
    grads = [grads[parts - 1]] + routed + [close]

    grad_query, grad_key, grad_value = attention_backward(
        place, probs, query2, key2, value2, attended, grads
    )
    received = jnp.concatenate(received, axis=0)
    grad_hidden = lax.dynamic_update_slice_in_dim(grad_hidden, received, (1 - branch) * half, 1)
    return (
        grad_hidden.reshape(hidden.shape),
        grad_query.reshape(query.shape),
        grad_key.reshape(key.shape),
        grad_value.reshape(value.shape),
        down_gradient_rows.T,
        adapter_up_gradient,
    )


def solution(mesh):
    in_specs = (
        P("branch", "fsdp", "ulysses", None),
        P("branch", "fsdp", None, "ulysses"),
        P("branch", "fsdp", None, "ulysses"),
        P("branch", "fsdp", None, "ulysses"),
        P("fsdp", None),
        P(),
        P(),
        P("fsdp", "ulysses", None),
    )
    out_specs = (
        P("branch", "fsdp", "ulysses", None),
        P("branch", "fsdp", None, "ulysses"),
        P("branch", "fsdp", None, "ulysses"),
        P("branch", "fsdp", None, "ulysses"),
        P(),
        P(),
    )
    return jax.shard_map(body, mesh=mesh, in_specs=in_specs, out_specs=out_specs, check_vma=False)
```

```python
import functools

import jax
import jax.numpy as jnp
from jax import lax
from jax.experimental import pallas as pl
from jax.experimental.pallas import tpu as pltpu
from jax.sharding import PartitionSpec as P

HD = 128
GUIDANCE = 5.0
SCALE = HD ** (-0.5)
VMEM = 56 * 1024 * 1024
LAST = (((1,), (1,)), ((), ()))
FIRST = (((0,), (0,)), ((), ()))
F32 = jnp.float32
BF16 = jnp.bfloat16


def lasts(us):
    return pl.CostEstimate(flops=1000, bytes_accessed=int(us * 3.69e6), transcendentals=0)


def dot(a, b, dims=(((1,), (0,)), ((), ()))):
    return lax.dot_general(a, b, dims, preferred_element_type=F32)


def params():
    return pltpu.CompilerParams(vmem_limit_bytes=VMEM)


def forward_kernel(q_ref, k_ref, v_ref, p_ref, o_ref):
    rows = o_ref.shape[2]
    for part in range(o_ref.shape[1]):
        at = pl.ds(part * rows, rows)
        scores = dot(k_ref[...], q_ref[at, :], LAST) * SCALE
        exps = jnp.exp(scores - jnp.max(scores, axis=0, keepdims=True))
        probs = (exps * (1.0 / jnp.sum(exps, axis=0, keepdims=True))).astype(BF16)
        p_ref[0, :, at] = probs
        out = dot(probs, v_ref[...], FIRST).astype(BF16)
        o_ref[0, part] = out
        o_ref[1, part] = out


def attention_forward(query, key, value, parts):
    seq, width = query.shape
    heads = width // HD
    block = pl.BlockSpec((seq, HD), lambda h: (0, h))
    return pl.pallas_call(
        forward_kernel,
        grid=(heads,),
        in_specs=[block] * 3,
        out_specs=[
            pl.BlockSpec((1, seq, seq), lambda h: (h, 0, 0)),
            pl.BlockSpec((2, parts, seq // parts, HD), lambda h: (0, 0, 0, h)),
        ],
        out_shape=[
            jax.ShapeDtypeStruct((heads, seq, seq), BF16),
            jax.ShapeDtypeStruct((2, parts, seq // parts, width), BF16),
        ],
        compiler_params=params(),
        cost_estimate=lasts(16),
    )(query, key, value)


def backward_kernel(u_ref, p_ref, q_ref, k_ref, v_ref, o_ref, *refs):
    (*g_refs, dq_ref, dk_ref, dv_ref, g_scr) = refs
    parts = len(g_refs) - 1
    rows, size = g_refs[0].shape
    for ahead in range(parts):
        part = lax.rem(u_ref[0] + (parts - ahead), parts)
        block = g_refs[ahead][...]
        if ahead == 0:
            block = (block.astype(F32) + g_refs[parts][...].astype(F32)).astype(BF16)
        g_scr[pl.ds(pl.multiple_of(part * rows, rows), rows), :] = block
    probs = p_ref[0]
    grad = g_scr[...]
    out = o_ref[0].reshape(parts * rows, size)
    delta = jnp.sum((grad.astype(F32) * out.astype(F32)).T, axis=0, keepdims=True)
    grad_probs = dot(v_ref[...], grad, LAST)
    grad_scores = (probs.astype(F32) * (grad_probs - delta)).astype(BF16)
    dv_ref[...] = dot(probs, grad).astype(BF16)
    dk_ref[...] = (dot(grad_scores, q_ref[...]) * SCALE).astype(BF16)
    dq_ref[...] = (dot(k_ref[...].T, grad_scores) * SCALE).T.astype(BF16)


def attention_backward(place, probs, query, key, value, out, grads):
    seq, width = query.shape
    heads = width // HD
    parts = out.shape[1]
    block = pl.BlockSpec((seq, HD), lambda h, u: (0, h))
    return pl.pallas_call(
        backward_kernel,
        grid_spec=pltpu.PrefetchScalarGridSpec(
            num_scalar_prefetch=1,
            grid=(heads,),
            in_specs=[
                pl.BlockSpec((1, seq, seq), lambda h, u: (h, 0, 0)),
                block,
                block,
                block,
                pl.BlockSpec((1, parts, seq // parts, HD), lambda h, u: (0, 0, 0, h)),
            ]
            + [pl.BlockSpec((seq // parts, HD), lambda h, u: (0, h))] * (parts + 1),
            out_specs=[block] * 3,
            scratch_shapes=[pltpu.VMEM((seq, HD), BF16)],
        ),
        out_shape=[jax.ShapeDtypeStruct((seq, width), BF16)] * 3,
        compiler_params=params(),
        cost_estimate=lasts(400),
    )(place, probs, query, key, value, out, *grads)


def weight_rows(w_ref):
    blocks = []
    for z in range(0, w_ref.shape[0], 4):
        blocks += [w_ref[z], w_ref[z + 2], w_ref[z + 1], w_ref[z + 3]]
    return jnp.concatenate(blocks, axis=0)


def velocity_kernel(
    b_ref, x_ref, m_ref, w_ref, hown_ref, hoth_ref, hlate_ref, r_ref, up_ref, v_ref, sum_ref, s_scr
):
    step = pl.program_id(0)
    tokens = hown_ref.shape[0]

    @pl.when(step == 0)
    def _():
        s_scr[...] = jnp.zeros_like(s_scr)

    first = b_ref[0] == 0
    own = hown_ref[...].astype(F32)
    oth = jnp.concatenate([hoth_ref[...], hlate_ref[...]], axis=0).astype(F32)
    acc = dot(x_ref[...], weight_rows(w_ref)) + dot(m_ref[...], up_ref[...])
    cond = (jnp.where(first, own, oth) + acc[:tokens]).astype(BF16)
    uncond = (jnp.where(first, oth, own) + acc[tokens:]).astype(BF16)
    v_ref[0] = cond
    v_ref[1] = uncond
    c32, u32, r32 = cond.astype(F32), uncond.astype(F32), r_ref[...].astype(F32)
    for row, term in enumerate((c32 * u32, u32 * u32, r32 * u32)):
        s_scr[pl.ds(row, 1), :] += jnp.sum(term, axis=0, keepdims=True)

    @pl.when(step == pl.num_programs(0) - 1)
    def _():
        totals = jnp.sum(s_scr[...], axis=1, keepdims=True)
        lane = lax.broadcasted_iota(jnp.int32, sum_ref.shape, 1)
        sum_ref[...] = jnp.where(
            lane == 0, totals[0:1], jnp.where(lane == 1, totals[1:2], totals[2:3])
        )


def velocity(branch, attended, middle, weight, hidden, hidden_other, reward, up, copies):
    half = weight.shape[2]
    tokens = hidden.shape[0]
    blocks, block_rows, _ = weight.shape
    depth, rank = blocks * block_rows, up.shape[0]
    tile = 512
    steps = half // tile
    mine = lambda j, b: (0, b[0] * steps + j)
    return pl.pallas_call(
        velocity_kernel,
        grid_spec=pltpu.PrefetchScalarGridSpec(
            num_scalar_prefetch=1,
            grid=(steps,),
            in_specs=[
                pl.BlockSpec((2 * tokens, depth), lambda j, b: (0, 0)),
                pl.BlockSpec((2 * tokens, rank), lambda j, b: (0, 0)),
                pl.BlockSpec((blocks, block_rows, tile), lambda j, b: (0, 0, j)),
                pl.BlockSpec((tokens, tile), mine),
                pl.BlockSpec((hidden_other[0].shape[0], tile), lambda j, b: (0, j)),
                pl.BlockSpec((hidden_other[1].shape[0], tile), lambda j, b: (0, j)),
                pl.BlockSpec((tokens, tile), mine),
                pl.BlockSpec((rank, tile), mine),
            ],
            out_specs=[
                pl.BlockSpec((2, tokens, tile), lambda j, b: (0, 0, j)),
                pl.BlockSpec((8 * copies, 128), lambda j, b: (0, 0)),
            ],
            scratch_shapes=[pltpu.VMEM((8, tile), F32)],
        ),
        out_shape=[
            jax.ShapeDtypeStruct((2, tokens, half), BF16),
            jax.ShapeDtypeStruct((8 * copies, 128), F32),
        ],
        compiler_params=params(),
        cost_estimate=lasts(14),
    )(branch, attended, middle, weight, hidden, *hidden_other, reward, up)


def guidance_kernel(
    b_ref, v_ref, r_ref, sum_ref, x_ref, m_ref, up_ref,
    own_ref, mid_ref, both_ref, *refs,
):
    step = pl.program_id(0)
    tokens, tile = r_ref.shape
    (*cut_refs, m_scr) = refs
    groups = both_ref.shape[0] // 2
    totals = sum_ref[0:1, :]
    for at in range(8, sum_ref.shape[0], 8):
        totals = totals + sum_ref[at : at + 1, :]
    inner, energy, pull = totals[:, 0:1], totals[:, 1:2] + 1e-08, totals[:, 2:3]
    scale = inner / energy
    slope = (1.0 - GUIDANCE) * pull / energy
    first = b_ref[0] == 0
    target = r_ref[...].astype(F32)
    cond = v_ref[0].astype(F32)
    uncond = v_ref[1].astype(F32)
    grad0 = (GUIDANCE * target + slope * uncond).astype(BF16)
    grad1 = (
        ((1.0 - GUIDANCE) * scale) * target
        + slope * cond
        + (-2.0 * slope * scale) * uncond
    ).astype(BF16)
    own_ref[...] = jnp.where(first, grad0, grad1)
    other = jnp.where(first, grad1, grad0)
    at = 0
    for cut_ref in cut_refs:
        cut_ref[...] = other[at : at + cut_ref.shape[0]]
        at += cut_ref.shape[0]
    up = up_ref[...]
    part = jnp.concatenate([dot(grad0, up, LAST), dot(grad1, up, LAST)], axis=0)
    up_part = dot(m_ref[:tokens], grad0, FIRST) + dot(m_ref[tokens:], grad1, FIRST)
    up_part = up_part.astype(BF16)
    for row in range(groups):
        both_ref[groups + row, step] = up_part[16 * row : 16 * row + 16]

    @pl.when(step == 0)
    def _():
        m_scr[...] = part

    @pl.when(step > 0)
    def _():
        m_scr[...] += part

    @pl.when(step == pl.num_programs(0) - 1)
    def _():
        mid = m_scr[...].astype(BF16)
        mid_ref[0:tokens] = jnp.where(first, mid[:tokens], mid[tokens:])
        mid_ref[tokens:] = jnp.where(first, mid[tokens:], mid[:tokens])
        down_part = dot(mid, x_ref[...], FIRST).astype(BF16)
        for row in range(groups):
            for lane in range(both_ref.shape[1]):
                both_ref[row, lane] = down_part[
                    16 * row : 16 * row + 16, lane * tile : lane * tile + tile
                ]


def guidance(branch, vel, reward, sums, attended, middle, up, cuts):
    _, tokens, half = vel.shape
    rank, depth = up.shape[0], attended.shape[1]
    tile = 640
    steps = half // tile
    whole = lambda j, b: (0, 0)
    mine = lambda j, b: (0, b[0] * steps + j)
    here = lambda j, b: (0, j)
    both = (2 * rank // 16, steps, 16, tile)
    return pl.pallas_call(
        guidance_kernel,
        grid_spec=pltpu.PrefetchScalarGridSpec(
            num_scalar_prefetch=1,
            grid=(steps,),
            in_specs=[
                pl.BlockSpec((2, tokens, tile), lambda j, b: (0, 0, j)),
                pl.BlockSpec((tokens, tile), mine),
                pl.BlockSpec(sums.shape, whole),
                pl.BlockSpec((2 * tokens, depth), whole),
                pl.BlockSpec((2 * tokens, rank), whole),
                pl.BlockSpec((rank, tile), mine),
            ],
            out_specs=[
                pl.BlockSpec((tokens, tile), mine),
                pl.BlockSpec((2 * tokens, rank), whole),
                pl.BlockSpec(both, lambda j, b: (0, 0, 0, 0)),
            ]
            + [pl.BlockSpec((cut, tile), here) for cut in cuts],
            scratch_shapes=[pltpu.VMEM((2 * tokens, rank), F32)],
        ),
        out_shape=[
            jax.ShapeDtypeStruct((tokens, 2 * half), BF16),
            jax.ShapeDtypeStruct((2 * tokens, rank), BF16),
            jax.ShapeDtypeStruct(both, BF16),
        ]
        + [jax.ShapeDtypeStruct((cut, half), BF16) for cut in cuts],
        compiler_params=params(),
        cost_estimate=lasts(8),
    )(branch, vel, reward, sums, attended, middle, up)


def gradient_kernel(u_ref, b_ref, own_ref, early_ref, late_ref, mid_ref, w_ref, down_ref, *refs):
    step = pl.program_id(0)
    tokens = own_ref.shape[0]
    rows = jnp.concatenate([own_ref[...], early_ref[...], late_ref[...]], axis=0)
    part = dot(rows, weight_rows(w_ref), LAST) + dot(mid_ref[...], down_ref[...])
    part = part.astype(BF16)
    *gown_refs, far_ref, near_ref = refs
    last = len(gown_refs) - 1
    for at in range(last + 1):

        @pl.when(step == at)
        def _():
            gown_refs[at][...] = part[:tokens]
            if at < last:
                far_ref[at * tokens : (at + 1) * tokens] = part[tokens:]
            else:
                near_ref[...] = part[tokens:]


def gradient(place, branch, grad_own, early, late, grad_middle, weight, down_rows, parts):
    tokens, half = grad_own.shape[0], late.shape[1]
    blocks, block_rows, _ = weight.shape
    rank, depth = down_rows.shape
    wide = depth // parts
    whole = lambda j, u, b: (0, 0)
    there = lambda j, u: lax.rem(u[0] + 1 + j, parts)
    return pl.pallas_call(
        gradient_kernel,
        grid_spec=pltpu.PrefetchScalarGridSpec(
            num_scalar_prefetch=2,
            grid=(parts,),
            in_specs=[
                pl.BlockSpec((tokens, half), lambda j, u, b: (0, b[0])),
                pl.BlockSpec(early.shape, whole),
                pl.BlockSpec(late.shape, whole),
                pl.BlockSpec((2 * tokens, rank), whole),
                pl.BlockSpec(
                    (blocks // parts, block_rows, half), lambda j, u, b: (there(j, u), 0, 0)
                ),
                pl.BlockSpec((rank, wide), lambda j, u, b: (0, there(j, u))),
            ],
            out_specs=[pl.BlockSpec((tokens, wide), whole)] * parts
            + [
                pl.BlockSpec(((parts - 1) * tokens, wide), whole),
                pl.BlockSpec((tokens, wide), whole),
            ],
        ),
        out_shape=[jax.ShapeDtypeStruct((tokens, wide), BF16)] * parts
        + [
            jax.ShapeDtypeStruct(((parts - 1) * tokens, wide), BF16),
            jax.ShapeDtypeStruct((tokens, wide), BF16),
        ],
        compiler_params=params(),
        cost_estimate=lasts(14),
    )(place, branch, grad_own, early, late, grad_middle, weight, down_rows)


def adapter_kernel(p_ref, down_ref, up_ref):
    members, _, _, rows, tile = p_ref.shape
    half = down_ref.shape[1]
    lanes = half // tile

    @pl.when(pl.program_id(0) < pl.num_programs(0) // 2)
    def _():
        for c in range(members):
            row, lane = divmod(c, lanes)
            both = p_ref[c, 0, 0].astype(F32) + p_ref[c, 0, 1].astype(F32)
            down_ref[pl.ds(row * rows, rows), pl.ds(lane * tile, tile)] = both

    @pl.when(pl.program_id(0) >= pl.num_programs(0) // 2)
    def _():
        for c in range(members):
            row, lane = divmod(c, lanes)
            for b in range(2):
                columns = pl.ds(b * half + lane * tile, tile)
                up_ref[pl.ds(row * rows, rows), columns] = p_ref[c, 0, b].astype(F32)


def adapter(pieces, rank, lanes):
    members, parts, _, rows, tile = pieces.shape
    half = lanes * tile
    span = members // lanes * rows
    first_up = parts // 2
    return pl.pallas_call(
        adapter_kernel,
        grid=(parts,),
        out_shape=[
            jax.ShapeDtypeStruct((rank, half), F32),
            jax.ShapeDtypeStruct((rank, 2 * half), F32),
        ],
        in_specs=[pl.BlockSpec((members, 1, 2, rows, tile), lambda u: (0, u, 0, 0, 0))],
        out_specs=[
            pl.BlockSpec((span, half), lambda u: (jnp.minimum(u, first_up - 1), 0)),
            pl.BlockSpec((span, 2 * half), lambda u: (jnp.maximum(u - first_up, 0), 0)),
        ],
        compiler_params=params(),
        cost_estimate=lasts(3),
    )(pieces)


def exchange(block, axes):
    return lax.all_to_all(block, axes, split_axis=0, concat_axis=0, tiled=True)


def swap(block):
    return lax.ppermute(block, "branch", [(0, 1), (1, 0)])


def ahead_send(block, ahead):
    parts = lax.axis_size("ulysses")
    return lax.ppermute(block, "ulysses", [(u, (u + ahead) % parts) for u in range(parts)])


def send_x(block, step):
    clips = lax.axis_size("fsdp")
    route = []
    for at in range(2 * clips):
        b, f = divmod(at, clips)
        z, rest = divmod(f, 4)
        near, core = divmod(rest, 2)
        x = (b * 2 + near + step) % 4
        route.append((at, (x // 2) * clips + z * 4 + (x % 2) * 2 + core))
    return lax.ppermute(block, ("branch", "fsdp"), route)


def gather_operand(rows, branch, half):
    near = lax.rem(lax.axis_index("fsdp") // 2, 2)
    top = rows.shape[0] // 2
    columns = lambda part, b: lax.dynamic_slice_in_dim(part, b * half, half, 1)
    forward = jnp.where(near == 0, branch, 1 - branch)
    before = send_x(columns(rows[:top], forward), 1)
    after = send_x(columns(rows[top:], 1 - forward), -1)
    beside = jnp.concatenate([before, after], axis=0)
    mine = columns(rows, branch)
    return jnp.where(
        near == 0,
        jnp.concatenate([mine, beside], axis=0),
        jnp.concatenate([beside, mine], axis=0),
    )


def body(
    hidden,
    query,
    key,
    value,
    output_projection_weight,
    adapter_down_weight,
    adapter_up_weight,
    reward_gradient,
):
    parts = lax.axis_size("ulysses")
    clips = lax.axis_size("fsdp")
    branch = lax.axis_index("branch")
    branch_word = branch.reshape(1).astype(jnp.int32)
    place = lax.axis_index("ulysses").reshape(1).astype(jnp.int32)
    _, _, tokens, model = hidden.shape
    half = model // 2
    _, _, seq, width = query.shape
    depth, rank = adapter_down_weight.shape
    query2, key2, value2 = (a.reshape(seq, width) for a in (query, key, value))
    hidden2 = hidden.reshape(tokens, model)
    reward2 = reward_gradient.reshape(tokens, model)

    operand = gather_operand(output_projection_weight, branch, half)
    operand, query2, hidden_ready = lax.optimization_barrier((operand, query2, hidden2))
    weight_groups = [
        [z * 4 + near * 2 + core for z in range(clips // 4) for core in (0, 1)] for near in (0, 1)
    ]
    weight = lax.all_gather(operand, "fsdp", axis=0, tiled=True, axis_index_groups=weight_groups)
    weight = weight.reshape(clips, depth // clips, half)
    early = 5 * tokens // 8
    hidden_send = lax.dynamic_slice_in_dim(hidden_ready, (1 - branch) * half, half, 1)
    hidden_early = swap(hidden_send[:early])
    hidden_late = hidden_send[early:]

    probs, attended = attention_forward(query2, key2, value2, parts)
    attended, hidden_early = lax.optimization_barrier((attended, hidden_early))
    gathered = exchange(attended.reshape(2 * seq, width), ("branch", "ulysses"))
    gathered, hidden_late = lax.optimization_barrier((gathered, hidden_late))
    hidden_late = swap(hidden_late)
    gathered = gathered.reshape(2, parts, tokens, width).transpose(0, 2, 1, 3)
    gathered = gathered.reshape(2 * tokens, depth)
    middle = dot(gathered, adapter_down_weight).astype(BF16)

    vel, sums = velocity(
        branch_word, gathered, middle, weight, hidden2, (hidden_early, hidden_late), reward2,
        adapter_up_weight, 2 * parts,
    )
    sums = exchange(sums, ("branch", "ulysses"))
    cuts = (tokens // 2, tokens // 2)
    grad_hidden, grad_middle, both, *pieces_out = guidance(
        branch_word, vel, reward2, sums, gathered, middle, adapter_up_weight, cuts
    )
    received = [swap(pieces_out[0])]

    groups = [
        [u * clips + z * 4 + near * 2 + core for u in range(parts) for z in range(clips // 4) for core in (0, 1)]
        for near in (0, 1)
    ]
    spread = lambda block: lax.all_to_all(
        block, ("ulysses", "fsdp"), split_axis=0, concat_axis=0, tiled=True, axis_index_groups=groups
    )
    row_groups, lanes, rows, tile = both.shape
    pieces = row_groups * lanes
    down_rows = adapter_down_weight.T
    *grads, far, close = gradient(
        place, branch_word, grad_hidden, *pieces_out, grad_middle, weight, down_rows, parts
    )
    far = swap(far)
    both, grads[3], received[0] = lax.optimization_barrier((both, grads[3], received[0]))
    both = spread(both.reshape(pieces * rows, tile))
    total = jnp.sum(both.reshape(pieces, rows, tile).astype(F32), axis=0)
    beside = [send_x(total, step) for step in (1, 2, 3)]
    far, close, *beside = lax.optimization_barrier((far, close, *beside))
    close = swap(close)
    far = far.reshape(parts - 1, tokens, width)
    routed = [
        ahead_send((grads[at].astype(F32) + far[at].astype(F32)).astype(BF16), at + 1)
        for at in range(parts - 1)
    ]
    close, pieces_out[1], *routed = lax.optimization_barrier((close, pieces_out[1], *routed))
    received.append(swap(pieces_out[1]))

    near = lax.rem(lax.axis_index("fsdp") // 2, 2)
    own_total = total + jnp.where(near == 0, beside[2], beside[0])
    other_total = beside[1] + jnp.where(near == 0, beside[0], beside[2])
    total = jnp.where(
        branch == 0,
        jnp.concatenate([own_total, other_total]),
        jnp.concatenate([other_total, own_total]),
    ).astype(BF16)
    ring = [total] + [ahead_send(total, ahead) for ahead in range(1, parts)]
    ring = jnp.concatenate(ring[::-1] * 2, axis=0)
    column = lax.dynamic_slice_in_dim(
        ring, (parts - 1 - place[0]) * 2 * rows, parts * 2 * rows, 0
    )
    packed = lax.all_gather(column, "fsdp", axis=0, tiled=True, axis_index_groups=weight_groups)
    packed = packed.reshape(clips // 2, parts, 2, rows, tile)
    down_gradient_rows, adapter_up_gradient = adapter(packed, rank, lanes)
    grads = [grads[parts - 1]] + routed + [close]

    grad_query, grad_key, grad_value = attention_backward(
        place, probs, query2, key2, value2, attended, grads
    )
    received = jnp.concatenate(received, axis=0)
    grad_hidden = lax.dynamic_update_slice_in_dim(grad_hidden, received, (1 - branch) * half, 1)
    return (
        grad_hidden.reshape(hidden.shape),
        grad_query.reshape(query.shape),
        grad_key.reshape(key.shape),
        grad_value.reshape(value.shape),
        down_gradient_rows.T,
        adapter_up_gradient,
    )


def solution(mesh):
    in_specs = (
        P("branch", "fsdp", "ulysses", None),
        P("branch", "fsdp", None, "ulysses"),
        P("branch", "fsdp", None, "ulysses"),
        P("branch", "fsdp", None, "ulysses"),
        P("fsdp", None),
        P(),
        P(),
        P("fsdp", "ulysses", None),
    )
    out_specs = (
        P("branch", "fsdp", "ulysses", None),
        P("branch", "fsdp", None, "ulysses"),
        P("branch", "fsdp", None, "ulysses"),
        P("branch", "fsdp", None, "ulysses"),
        P(),
        P(),
    )
    return jax.shard_map(body, mesh=mesh, in_specs=in_specs, out_specs=out_specs, check_vma=False)
```
